512 devices in a mesh: inst: 64 (over z, x, core), tp: 8 (over y).
Axes of the slice: x: 4, y: 8, z: 8, core: 2. Of those that a mesh axis runs over, the one named last changes fastest.
Arguments:
- queries: bfloat16 [512, 8192], P('inst', 'tp'), may hold values from -4 to 4
- pool_keys: bfloat16 [2048, 128, 1024], P('inst', None, 'tp'), may hold values from -16 to 16
- pool_values: bfloat16 [2048, 128, 1024], P('inst', None, 'tp'), may hold values from -6 to 6
- block_table: int32 [512, 4], P('inst'), may hold values from 0 to 2047, as said below
- ctx_len: int32 [512], P('inst'), may hold values from 1 to 512, 196608 in all
- out_weight: bfloat16 [8192, 8192], P('tp', 'inst'), may hold values from -0.5 to 0.5
Outputs:
- layer_out: bfloat16 [512, 8192], P('tp', 'inst')
The draws below stay inside these ranges and needn't reach their ends.
Inputs may be any that keep to these rules, and one draw needn't show every extreme that they name: block_table[r, b] is the pool slot of block b of request r (entries past the request's length are still valid slots); every pool slot holds exactly one (request, block) entry of the table; instance i owns slots i * 32 to (i + 1) * 32 - 1 and request r has home instance r // 8. Of the 32 entries of one home's requests, at most 2 lie on any one instance; exactly 2 lie on the instance after the home (counted round), and some lie on the instance before it.
All inputs are finite; a program needn't handle non-finite values. No bound on the sum of `ctx_len` on one device may be relied on, other than what follows from the above.
Results may differ from the reference program's by a relative error of at most 0.005.
Values may be sent and summed in bfloat16 or wider, within the bound.
No kernel may reach another device: no remote copies, remote signals or barrier semaphores. Data moves between devices by JAX's collectives and lax.ppermute only.
A program may use at most 64 MiB of HBM per device.

```python
import math
from functools import partial
import jax
import jax.numpy as jnp
import numpy as np
from jax import lax

D = 8192
HQ = 64
KVH = 8
HD = 128
BLOCK = 128
MAXB = 4
REQ = 512
BLK_DEV = 32
POOL = 2048
CAP = 2
N_INST = 64


def draw_queries(key, part):
    key = jax.random.fold_in(key, 31)
    values = jnp.clip(jax.random.normal(key, (REQ, HQ, HD), jnp.float32), -4.0, 4.0)
    return values.reshape(REQ, HQ * HD).astype(jnp.bfloat16)


def draw_pool_keys(key, part):
    key = jax.random.fold_in(key, 32)
    scale_key, value_key = jax.random.split(key)
    spread = jnp.exp(jax.random.uniform(scale_key, (POOL, BLOCK, 1, 1), jnp.float32, math.log(0.3), math.log(3.0)))
    values = jnp.clip(jax.random.normal(value_key, (POOL, BLOCK, KVH, HD), jnp.float32), -4.0, 4.0) * spread
    return values.reshape(POOL, BLOCK, KVH * HD).astype(jnp.bfloat16)


def draw_block_table(key, part):
    key = jax.random.fold_in(key, 33)
    order_key, home_key = jax.random.split(key)
    others = jnp.asarray(np.concatenate([np.array([0], dtype=np.int32), np.arange(2, max(N_INST - 1, 2), dtype=np.int32)]))
    shuffled = jax.random.permutation(order_key, others)
    sigma = jnp.concatenate([jnp.asarray(np.array([1, (N_INST - 1) % N_INST], dtype=np.int32)), shuffled]).astype(jnp.int32)
    entries = jnp.arange(BLK_DEV, dtype=jnp.int32)
    spread_steps = max(BLK_DEV - CAP, 1)
    picks = jnp.where(entries < CAP, 0, 1 + (entries - CAP) * (N_INST - 1) // spread_steps)
    offsets = sigma[picks]
    home_keys = jax.random.split(home_key, N_INST)
    arrangement = jax.vmap(lambda single: jax.random.permutation(single, BLK_DEV))(home_keys)
    homes = jnp.arange(N_INST, dtype=jnp.int32)[:, None]
    table = (homes + offsets[arrangement]) % N_INST * BLK_DEV + arrangement
    return table.reshape(REQ, MAXB).astype(jnp.int32)


def block_scale(own_key, shape, cuts, low, top_value):
    level = 1.0
    for dim, parts in cuts:
        heights = jax.random.uniform(jax.random.fold_in(jax.random.fold_in(own_key, 6), dim), (parts,), jnp.float32, low / len(cuts), top_value / len(cuts))
        level = level * jnp.repeat(jnp.exp(heights), shape[dim] // parts).reshape((-1,) + (1,) * (len(shape) - 1 - dim))
    return level


def split_up(amount, total, reach, slope):
    loads = [(1 << 20) // math.isqrt(grade ** slope) + 1 for grade in range(2, amount + 1)]
    spare, given = total - reach - (amount - 1), [1] * (amount - 1)
    while spare > 0:
        candidates = [i for i in range(amount - 1) if given[i] < reach]
        pool, remaining = sum([loads[i] for i in candidates]), spare
        for i in candidates:
            addition = min(reach - given[i], max(1, remaining * loads[i] // pool), spare)
            given[i] = given[i] + addition
            spare = spare - addition
    return np.array([reach] + given)


def uneven_parts(stream_key, number_of, total, bound, skew):
    if number_of == 2:
        one = jax.random.randint(stream_key, (), max(1, total - bound), min(bound, total - 1) + 1)
        return jnp.stack([one, total - one])
    lengths = jnp.asarray(split_up(number_of, total, bound, skew), jnp.int32)
    twos = (number_of - 1) // 2
    giver, taker = lengths[1:1 + 2 * twos:2], lengths[2:2 + 2 * twos:2]
    slack = jnp.minimum(giver - 1, bound - taker)
    moved = jax.random.randint(jax.random.fold_in(stream_key, 1), (twos,), 0, 1 << 20) % (slack + 1)
    lengths = lengths.at[1:1 + 2 * twos:2].set(giver - moved).at[2:2 + 2 * twos:2].set(taker + moved)
    return lengths[jax.random.permutation(jax.random.fold_in(stream_key, 2), number_of)]


def scatter_about(own_key, extent, scale, reach, shards=(), kind=jnp.bfloat16):
    values = jax.random.normal(own_key, extent, jnp.float32) * scale
    if len(shards) > 0:
        values = block_scale(own_key, extent, shards, -0.22, 0.18) * values
    return jnp.clip(values, min=-reach, max=reach).astype(kind)


def setup_inputs(seed: int = 0) -> dict:
    key_list = jax.random.split(jax.random.key(seed), 7)
    return {
        "queries": draw_queries(jax.random.fold_in(key_list[6], 71), 0),
        "pool_keys": draw_pool_keys(jax.random.fold_in(key_list[6], 71), 0),
        "pool_values": scatter_about(key_list[2], (POOL, BLOCK, KVH * HD), 1.0, 6.0, ((0, 64), (2, 8))),
        "block_table": draw_block_table(jax.random.fold_in(key_list[6], 71), 0),
        "ctx_len": uneven_parts(key_list[4], REQ, REQ * MAXB * BLOCK * 3 // 4, MAXB * BLOCK, 1).astype(jnp.int32),
        "out_weight": scatter_about(key_list[5], (HQ * HD, D), (HQ * HD // 64) ** -0.5, 0.5, ((0, 8), (1, 64))),
    }


very_low = -1.0e30


def request_attention(pool_keys, pool_values, inputs):
    q_row, table_row, length = inputs
    per_group = HQ // KVH
    q_heads = q_row.astype(jnp.float32).reshape(KVH, per_group, HD)
    key_rows = pool_keys[table_row].astype(jnp.float32).reshape(MAXB, BLOCK, KVH, HD)
    value_rows = pool_values[table_row].astype(jnp.float32).reshape(MAXB, BLOCK, KVH, HD)
    scores = jnp.einsum("kgd,btkd->bkgt", q_heads, key_rows) * (HD ** -0.5)
    counts = jnp.clip(length - jnp.arange(MAXB, dtype=jnp.int32) * BLOCK, 0, BLOCK)
    usable = jnp.arange(BLOCK, dtype=jnp.int32)[None, None, None, :] < counts[:, None, None, None]
    scores = jnp.where(usable, scores, very_low)
    maxima = jnp.max(scores, axis=3)
    weights = jnp.where(usable, jnp.exp(scores - maxima[..., None]), 0.0)
    totals = jnp.sum(weights, axis=3)
    rounded = lax.optimization_barrier(weights.astype(jnp.bfloat16)).astype(jnp.float32)
    block_out = jnp.einsum("bkgt,btkd->bkgd", rounded, value_rows)
    is_live = counts > 0
    top = jnp.max(maxima, axis=0)
    factor = jnp.where(is_live[:, None, None], jnp.exp(maxima - top[None]), 0.0)
    total = jnp.sum(factor * totals, axis=0)
    merged = jnp.sum(factor[..., None] * block_out, axis=0)
    return (merged / total[..., None]).reshape(HQ * HD).astype(jnp.bfloat16)


def reference(queries, pool_keys, pool_values, block_table, ctx_len, out_weight):
    attention = lax.map(partial(request_attention, pool_keys, pool_values), (queries, block_table, ctx_len))
    return jnp.dot(attention, out_weight, preferred_element_type=jnp.float32).astype(jnp.bfloat16)
```

```python
import jax
import jax.numpy as jnp
from jax import lax
from jax.experimental import pallas as pl
from jax.experimental.pallas import tpu as pltpu
from jax.sharding import Mesh, PartitionSpec as P

HD = 128
BLOCK = 128
MAXB = 4
SLOTS = 32
HEADS = 8
REQS = 8
PEERS = 64
MSG = 24
very_low = -1e30
f32 = jnp.float32
bf16 = jnp.bfloat16

VMEM = pl.BlockSpec(memory_space=pltpu.VMEM)
SMEM = pl.BlockSpec(memory_space=pltpu.SMEM)


def route_kernel(table, ctx, q, out, where_to, buf, rows, used):
    buf[...] = jnp.zeros_like(buf)
    for p in range(PEERS):
        used[p] = 0
    whole = q[...].astype(f32)
    for h in range(HEADS):
        rows[pl.ds(h, REQS, stride=HEADS), :] = whole[:, h * HD : (h + 1) * HD]
    lane = lax.broadcasted_iota(jnp.int32, (HEADS, HD), 1)
    for e in range(REQS * MAXB):
        r, b = e // MAXB, e % MAXB
        slot = table[r, b]
        p = slot >> 5
        pos = used[p]
        used[p] = pos + 1
        count = jnp.clip(ctx[r] - b * BLOCK, 0, BLOCK)
        where_to[e] = p * 2 + pos
        buf[pl.ds(pl.multiple_of(p * MSG + pos * 8, 8), 8), :] = rows[r * 8 : r * 8 + 8, :]
        meta = pl.ds(pl.multiple_of(p * MSG + 16, 8), 8)
        note = jnp.where(lane == 2 * pos, (slot & 31) + 1, jnp.where(lane == 2 * pos + 1, count, 0))
        buf[meta, :] = buf[meta, :] + note.astype(f32)
    out[...] = buf[...].astype(bf16)


def attend_kernel(items, keys, values, out):
    got = items[...].astype(f32).reshape(PEERS, 3, 8, HD)
    meta = got[:, 2]
    lane = lax.broadcasted_iota(jnp.int32, (PEERS, 8, SLOTS * HEADS), 2)
    head = lax.broadcasted_iota(jnp.int32, (PEERS, 8, SLOTS * HEADS), 1)
    same_head = (lane & 7) == head
    slot_no = ((lane >> 3) + 1).astype(f32)
    picks, sides = [], []
    for pos in range(2):
        slot = meta[:, :, 2 * pos : 2 * pos + 1]
        count = meta[:, :, 2 * pos + 1 : 2 * pos + 2]
        pick = jnp.where(same_head & (slot_no == slot), 1.0, 0.0)
        picks.append(pick.reshape(PEERS * 8, SLOTS * HEADS).astype(bf16))
        counts = jnp.broadcast_to(count, (PEERS, 8, HD)).reshape(PEERS * 8, HD)
        sides.append(
            jnp.concatenate([got[:, pos].reshape(PEERS * 8, HD), counts], axis=1).astype(bf16)
        )
    by_slot = lax.dot_general(
        jnp.concatenate(picks, axis=0),
        jnp.concatenate(sides, axis=0),
        (((0,), (0,)), ((), ())),
        preferred_element_type=f32,
    )
    query, counts = by_slot[:, :HD], by_slot[:, HD:]
    parts = []
    for s in range(0, SLOTS, 2):
        pair = lax.dot_general(
            query[s * 8 : s * 8 + 16].astype(bf16),
            keys[s : s + 2].reshape(2 * BLOCK, HD),
            (((1,), (1,)), ((), ())),
            preferred_element_type=f32,
        )
        parts += [pair[:8, :BLOCK], pair[8:, BLOCK:]]
    scores = jnp.concatenate(parts, axis=0) * HD ** (-0.5)
    token = lax.broadcasted_iota(jnp.int32, scores.shape, 1).astype(f32)
    usable = token < counts
    scores = jnp.where(usable, scores, very_low)
    top = jnp.max(scores, axis=1, keepdims=True)
    weights = jnp.where(usable, jnp.exp(scores - top), 0.0)
    total = jnp.sum(weights, axis=1, keepdims=True)
    none = jnp.zeros((8, BLOCK), f32)
    parts = []
    for s in range(0, SLOTS, 2):
        first = jnp.concatenate([weights[s * 8 : s * 8 + 8], none], axis=1)
        second = jnp.concatenate([none, weights[s * 8 + 8 : s * 8 + 16]], axis=1)
        parts.append(
            jnp.dot(
                jnp.concatenate([first, second], axis=0).astype(bf16),
                values[s : s + 2].reshape(2 * BLOCK, HD),
                preferred_element_type=f32,
            )
        )
    output = jnp.concatenate(parts, axis=0)
    alive = total > 0.0
    safe = jnp.where(alive, total, 1.0)
    output = (output / safe).astype(bf16)
    lse = jnp.where(alive, top + jnp.log(safe), very_low)
    high = lse.astype(bf16).astype(f32)
    mid = (lse - high).astype(bf16).astype(f32)
    low = lse - high - mid
    at = lax.broadcasted_iota(jnp.int32, (SLOTS * HEADS, HD), 1)
    back = []
    for pos in range(2):
        note = jnp.where(
            at == 3 * pos,
            high,
            jnp.where(at == 3 * pos + 1, mid, jnp.where(at == 3 * pos + 2, low, 0.0)),
        )
        side = jnp.concatenate([output, note.astype(bf16)], axis=1)
        back.append(jnp.dot(picks[pos], side, preferred_element_type=f32))
    notes = back[0][:, HD:] + back[1][:, HD:]
    tiles = [v.reshape(PEERS, 1, 8, HD) for v in (back[0][:, :HD], back[1][:, :HD], notes)]
    out[...] = jnp.concatenate(tiles, axis=1).reshape(PEERS * MSG, HD).astype(bf16)


def merge_kernel(where_to, items, out, got, rows):
    got[...] = items[...].astype(f32)
    lane = lax.broadcasted_iota(jnp.int32, (HEADS, HD), 1)
    for r in range(REQS):
        outs, lses = [], []
        for b in range(MAXB):
            item = where_to[r * MAXB + b]
            p, pos = item >> 1, item & 1
            outs.append(got[pl.ds(pl.multiple_of(p * MSG + pos * 8, 8), 8), :])
            note = got[pl.ds(pl.multiple_of(p * MSG + 16, 8), 8), :]
            mine = (lane >= 3 * pos) & (lane < 3 * pos + 3)
            lses.append(jnp.sum(jnp.where(mine, note, 0.0), axis=1, keepdims=True))
        top = jnp.maximum(jnp.maximum(lses[0], lses[1]), jnp.maximum(lses[2], lses[3]))
        scales = [jnp.exp(v - top) for v in lses]
        total = scales[0] + scales[1] + scales[2] + scales[3]
        merged = sum(s * o for s, o in zip(scales, outs))
        rows[r * 8 : r * 8 + 8, :] = merged / total
    whole = jnp.concatenate(
        [rows[pl.ds(h, REQS, stride=HEADS), :] for h in range(HEADS)], axis=1
    )
    out[...] = jnp.concatenate([whole] * 8, axis=0).astype(bf16)


def project_kernel(attention, weight, out):
    left = attention[...]
    for n in range(8):
        part = jnp.dot(left, weight[n], preferred_element_type=f32)
        out[n * 64 : (n + 1) * 64, :] = part.astype(bf16)


def total_kernel(parts, out):
    got = parts[...].astype(f32).reshape(8, 8, 8, HD)
    out[...] = jnp.sum(got, axis=1).reshape(64, HD).astype(bf16)


def per_device(queries, pool_keys, pool_values, block_table, ctx_len, out_weight):
    inst = ("z", "x", "c")
    limit = pltpu.CompilerParams(vmem_limit_bytes=24 * 1024 * 1024)
    weights = lax.all_gather(out_weight, ("x", "c"), axis=0, tiled=False)
    send, where_to = pl.pallas_call(
        route_kernel,
        out_shape=(
            jax.ShapeDtypeStruct((PEERS * MSG, HD), bf16),
            jax.ShapeDtypeStruct((REQS * MAXB,), jnp.int32),
        ),
        in_specs=[SMEM, SMEM, VMEM],
        out_specs=(VMEM, SMEM),
        scratch_shapes=[
            pltpu.VMEM((PEERS * MSG, HD), f32),
            pltpu.VMEM((REQS * HEADS, HD), f32),
            pltpu.SMEM((PEERS,), jnp.int32),
        ],
        compiler_params=limit,
        name="route",
    )(block_table, ctx_len, queries)
    items = lax.all_to_all(
        send.reshape(PEERS, MSG, HD), inst, split_axis=0, concat_axis=0, tiled=True
    )
    back = pl.pallas_call(
        attend_kernel,
        out_shape=jax.ShapeDtypeStruct((PEERS * MSG, HD), bf16),
        in_specs=[VMEM, VMEM, VMEM],
        out_specs=VMEM,
        compiler_params=limit,
        name="attend",
    )(items.reshape(PEERS * MSG, HD), pool_keys, pool_values)
    partials = lax.all_to_all(
        back.reshape(PEERS, MSG, HD), inst, split_axis=0, concat_axis=0, tiled=True
    )
    attention = pl.pallas_call(
        merge_kernel,
        out_shape=jax.ShapeDtypeStruct((8 * REQS, HEADS * HD), bf16),
        in_specs=[SMEM, VMEM],
        out_specs=VMEM,
        scratch_shapes=[
            pltpu.VMEM((PEERS * MSG, HD), f32),
            pltpu.VMEM((REQS * HEADS, HD), f32),
        ],
        compiler_params=limit,
        name="merge",
    )(where_to, partials.reshape(PEERS * MSG, HD))
    gathered = lax.all_to_all(
        attention.reshape(8, REQS, HEADS * HD), "z", split_axis=0, concat_axis=0, tiled=True
    )
    parts = pl.pallas_call(
        project_kernel,
        out_shape=jax.ShapeDtypeStruct((512, HD), bf16),
        in_specs=[VMEM, VMEM],
        out_specs=VMEM,
        compiler_params=limit,
        name="project",
    )(gathered.reshape(64, HEADS * HD), weights)
    swapped = lax.all_to_all(
        parts.reshape(64, 8, HD), ("x", "c", "tp"), split_axis=0, concat_axis=0, tiled=True
    )
    return pl.pallas_call(
        total_kernel,
        out_shape=jax.ShapeDtypeStruct((64, HD), bf16),
        in_specs=[VMEM],
        out_specs=VMEM,
        name="total",
    )(swapped.reshape(512, HD))


def solution(mesh):
    split = Mesh(mesh.devices.reshape(8, 4, 2, 8), ("z", "x", "c", "tp"))
    inst = ("z", "x", "c")
    in_specs = (
        P(inst, "tp"),
        P(inst, None, "tp"),
        P(inst, None, "tp"),
        P(inst, None),
        P(inst),
        P("tp", inst),
    )
    return jax.shard_map(
        per_device, mesh=split, in_specs=in_specs, out_specs=P("tp", inst), check_vma=False
    )
```

```python
import jax
import jax.numpy as jnp
from jax import lax
from jax.experimental import pallas as pl
from jax.experimental.pallas import tpu as pltpu
from jax.sharding import Mesh, PartitionSpec as P

HD = 128
BLOCK = 128
MAXB = 4
SLOTS = 32
HEADS = 8
REQS = 8
PEERS = 64
MSG = 18
very_low = -1e30
f32 = jnp.float32
bf16 = jnp.bfloat16

VMEM = pl.BlockSpec(memory_space=pltpu.VMEM)
SMEM = pl.BlockSpec(memory_space=pltpu.SMEM)
HBM = pl.BlockSpec(memory_space=pltpu.HBM)
limit = pltpu.CompilerParams(vmem_limit_bytes=24 * 1024 * 1024)


def route_kernel(table_in, ctx_in, q_in, out, where_to, table, ctx, q, buf, rows, used, sems):
    copies = [
        pltpu.make_async_copy(src, dst, sems.at[n])
        for n, (src, dst) in enumerate(((table_in, table), (ctx_in, ctx), (q_in, q)))
    ]
    for copy in copies:
        copy.start()
    buf[...] = jnp.zeros_like(buf)
    for p in range(PEERS):
        used[p] = 0
    for copy in copies:
        copy.wait()
    whole = q[...].astype(f32)
    for h in range(HEADS):
        rows[pl.ds(h, REQS, stride=HEADS), :] = whole[:, h * HD : (h + 1) * HD]
    lane = lax.broadcasted_iota(jnp.int32, (1, HD), 1)
    for e in range(REQS * MAXB):
        r, b = e // MAXB, e % MAXB
        slot = table[b, r]
        p = slot >> 5
        pos = used[p]
        used[p] = pos + 1
        count = jnp.clip(ctx[r] - b * BLOCK, 0, BLOCK)
        first = p * MSG + pos
        where_to[e] = first
        buf[pl.ds(first, HEADS, stride=2), :] = rows[r * 8 : r * 8 + 8, :]
        note = jnp.where(lane == 0, (slot & 31) + 1, jnp.where(lane == 1, count, 0))
        buf[pl.ds(first + 16, 1), :] = note.astype(f32)
    out[...] = buf[...].astype(bf16)


def attend_kernel(items, keys, values, out, buf, rows, counts):
    buf[...] = items[...].astype(f32)
    notes = jnp.concatenate([buf[pl.ds(16 + i, PEERS, stride=MSG), :] for i in range(2)], axis=0)
    queries = jnp.concatenate(
        [
            jnp.concatenate(
                [buf[pl.ds(2 * h + i, PEERS, stride=MSG), :] for h in range(HEADS)], axis=1
            )
            for i in range(2)
        ],
        axis=0,
    )
    slot_no = lax.broadcasted_iota(jnp.int32, (2 * PEERS, HD), 1).astype(f32) + 1.0
    pick = jnp.where(slot_no == notes[:, :1], 1.0, 0.0).astype(bf16)
    side = jnp.concatenate(
        [queries, jnp.broadcast_to(notes[:, 1:2], (2 * PEERS, HD))], axis=1
    ).astype(bf16)
    by_slot = lax.dot_general(
        pick, side, (((0,), (0,)), ((), ())), preferred_element_type=f32
    )[:SLOTS]
    for h in range(HEADS):
        rows[pl.ds(h, SLOTS, stride=HEADS), :] = by_slot[:, h * HD : (h + 1) * HD]
        counts[pl.ds(h, SLOTS, stride=HEADS), :] = by_slot[:, HEADS * HD :]
    parts = []
    for s in range(0, SLOTS, 2):
        pair = lax.dot_general(
            rows[s * 8 : s * 8 + 16, :].astype(bf16),
            keys[s : s + 2].reshape(2 * BLOCK, HD),
            (((1,), (1,)), ((), ())),
            preferred_element_type=f32,
        )
        parts += [pair[:8, :BLOCK], pair[8:, BLOCK:]]
    scores = jnp.concatenate(parts, axis=0) * HD ** (-0.5)
    token = lax.broadcasted_iota(jnp.int32, scores.shape, 1).astype(f32)
    usable = token < counts[...]
    scores = jnp.where(usable, scores, very_low)
    top = jnp.max(scores, axis=1, keepdims=True)
    weights = jnp.where(usable, jnp.exp(scores - top), 0.0)
    total = jnp.sum(weights, axis=1, keepdims=True)
    none = jnp.zeros((8, BLOCK), f32)
    parts = []
    for s in range(0, SLOTS, 2):
        first = jnp.concatenate([weights[s * 8 : s * 8 + 8], none], axis=1)
        second = jnp.concatenate([none, weights[s * 8 + 8 : s * 8 + 16]], axis=1)
        parts.append(
            jnp.dot(
                jnp.concatenate([first, second], axis=0).astype(bf16),
                values[s : s + 2].reshape(2 * BLOCK, HD),
                preferred_element_type=f32,
            )
        )
    alive = total > 0.0
    safe = jnp.where(alive, total, 1.0)
    rows[...] = jnp.concatenate(parts, axis=0) / safe
    lse = jnp.where(alive, top + jnp.log(safe), very_low)
    high = lse.astype(bf16).astype(f32)
    mid = (lse - high).astype(bf16).astype(f32)
    low = lse - high - mid
    lane = lax.broadcasted_iota(jnp.int32, (SLOTS * HEADS, HD), 1)
    head = lax.broadcasted_iota(jnp.int32, (SLOTS * HEADS, HD), 0) & 7
    note = jnp.where(
        lane == head,
        high,
        jnp.where(lane == head + 8, mid, jnp.where(lane == head + 16, low, 0.0)),
    )
    note = jnp.sum(note.reshape(SLOTS, HEADS, HD), axis=1)
    side = jnp.concatenate(
        [rows[pl.ds(h, SLOTS, stride=HEADS), :] for h in range(HEADS)] + [note], axis=1
    ).astype(bf16)
    back = jnp.dot(pick[:, :SLOTS], side, preferred_element_type=f32)
    for i in range(2):
        for j in range(HEADS + 1):
            buf[pl.ds(2 * j + i, PEERS, stride=MSG), :] = back[
                i * PEERS : (i + 1) * PEERS, j * HD : (j + 1) * HD
            ]
    out[...] = buf[...].astype(bf16)


def merge_kernel(where_to, items, out, got, rows):
    got[...] = items[...].astype(f32)
    lane = lax.broadcasted_iota(jnp.int32, (HEADS, HD), 1)
    head = lax.broadcasted_iota(jnp.int32, (HEADS, HD), 0)
    mine = ((lane & 7) == head) & (lane < 24)
    for r in range(REQS):
        outs, lses = [], []
        for b in range(MAXB):
            first = where_to[r * MAXB + b]
            outs.append(got[pl.ds(first, HEADS, stride=2), :])
            note = jnp.broadcast_to(got[pl.ds(first + 16, 1), :], (HEADS, HD))
            lses.append(jnp.sum(jnp.where(mine, note, 0.0), axis=1, keepdims=True))
        top = jnp.maximum(jnp.maximum(lses[0], lses[1]), jnp.maximum(lses[2], lses[3]))
        scales = [jnp.exp(v - top) for v in lses]
        total = scales[0] + scales[1] + scales[2] + scales[3]
        merged = sum(s * o for s, o in zip(scales, outs))
        rows[r * 8 : r * 8 + 8, :] = merged / total
    whole = jnp.concatenate(
        [rows[pl.ds(h, REQS, stride=HEADS), :] for h in range(HEADS)], axis=1
    )
    out[...] = jnp.concatenate([whole] * 8, axis=0).astype(bf16)


def stage_kernel(*refs):
    n = (len(refs) - 1) // 2
    sources, targets, sems = refs[:n], refs[n : 2 * n], refs[-1]
    copies = []
    for a in range(n):
        step = sources[a].shape[0] // 4
        for k in range(4):
            part = pl.ds(k * step, step)
            copies.append(
                pltpu.make_async_copy(sources[a].at[part], targets[a].at[part], sems.at[a * 4 + k])
            )
    for copy in copies:
        copy.start()
    for copy in copies:
        copy.wait()


def stage(*arrays, name):
    return pl.pallas_call(
        stage_kernel,
        out_shape=tuple(jax.ShapeDtypeStruct(a.shape, a.dtype) for a in arrays),
        in_specs=[HBM] * len(arrays),
        out_specs=(VMEM,) * len(arrays),
        scratch_shapes=[pltpu.SemaphoreType.DMA((4 * len(arrays),))],
        compiler_params=limit,
        cost_estimate=pl.CostEstimate(flops=0, bytes_accessed=1 << 22, transcendentals=0),
        name=name,
    )(*arrays)


def project_kernel(attention, weight, out):
    left = attention[...]
    for n in range(8):
        part = jnp.dot(left, weight[n], preferred_element_type=f32)
        out[n * 64 : (n + 1) * 64, :] = part.astype(bf16)


def total_kernel(parts, out):
    got = parts[...].astype(f32).reshape(8, 8, 8, HD)
    out[...] = jnp.sum(got, axis=1).reshape(64, HD).astype(bf16)


def per_device(queries, pool_keys, pool_values, block_table, ctx_len, out_weight):
    inst = ("z", "x", "c")
    send, where_to = pl.pallas_call(
        route_kernel,
        out_shape=(
            jax.ShapeDtypeStruct((PEERS * MSG, HD), bf16),
            jax.ShapeDtypeStruct((REQS * MAXB,), jnp.int32),
        ),
        in_specs=[HBM, HBM, HBM],
        out_specs=(VMEM, SMEM),
        scratch_shapes=[
            pltpu.SMEM((MAXB, REQS), jnp.int32),
            pltpu.SMEM((REQS,), jnp.int32),
            pltpu.VMEM((REQS, HEADS * HD), bf16),
            pltpu.VMEM((PEERS * MSG, HD), f32),
            pltpu.VMEM((REQS * HEADS, HD), f32),
            pltpu.SMEM((PEERS,), jnp.int32),
            pltpu.SemaphoreType.DMA((3,)),
        ],
        compiler_params=limit,
        name="route",
    )(block_table.T, ctx_len, queries)
    out_weight, send = lax.optimization_barrier((out_weight, send))
    weights = lax.all_gather(out_weight, ("x", "c"), axis=0, tiled=False)
    items = lax.all_to_all(
        send.reshape(PEERS, HEADS + 1, 2, HD), inst, split_axis=0, concat_axis=0, tiled=True
    )
    keys, values = stage(pool_keys, pool_values, name="stage_blocks")
    back = pl.pallas_call(
        attend_kernel,
        out_shape=jax.ShapeDtypeStruct((PEERS * MSG, HD), bf16),
        in_specs=[VMEM, VMEM, VMEM],
        out_specs=VMEM,
        scratch_shapes=[
            pltpu.VMEM((PEERS * MSG, HD), f32),
            pltpu.VMEM((SLOTS * HEADS, HD), f32),
            pltpu.VMEM((SLOTS * HEADS, HD), f32),
        ],
        compiler_params=limit,
        name="attend",
    )(items.reshape(PEERS * MSG, HD), keys, values)
    partials = lax.all_to_all(
        back.reshape(PEERS, HEADS + 1, 2, HD), inst, split_axis=0, concat_axis=0, tiled=True
    )
    attention = pl.pallas_call(
        merge_kernel,
        out_shape=jax.ShapeDtypeStruct((8 * REQS, HEADS * HD), bf16),
        in_specs=[SMEM, VMEM],
        out_specs=VMEM,
        scratch_shapes=[
            pltpu.VMEM((PEERS * MSG, HD), f32),
            pltpu.VMEM((REQS * HEADS, HD), f32),
        ],
        compiler_params=limit,
        name="merge",
    )(where_to, partials.reshape(PEERS * MSG, HD))
    (weights,) = stage(weights, name="stage_weights")
    gathered = lax.all_to_all(
        attention.reshape(8, REQS, HEADS * HD), "z", split_axis=0, concat_axis=0, tiled=True
    )
    parts = pl.pallas_call(
        project_kernel,
        out_shape=jax.ShapeDtypeStruct((512, HD), bf16),
        in_specs=[VMEM, VMEM],
        out_specs=VMEM,
        compiler_params=limit,
        name="project",
    )(gathered.reshape(64, HEADS * HD), weights)
    swapped = lax.all_to_all(
        parts.reshape(64, 8, HD), ("x", "c", "tp"), split_axis=0, concat_axis=0, tiled=True
    )
    return pl.pallas_call(
        total_kernel,
        out_shape=jax.ShapeDtypeStruct((64, HD), bf16),
        in_specs=[VMEM],
        out_specs=VMEM,
        name="total",
    )(swapped.reshape(512, HD))


def solution(mesh):
    split = Mesh(mesh.devices.reshape(8, 4, 2, 8), ("z", "x", "c", "tp"))
    inst = ("z", "x", "c")
    in_specs = (
        P(inst, "tp"),
        P(inst, None, "tp"),
        P(inst, None, "tp"),
        P(inst, None),
        P(inst),
        P("tp", inst),
    )
    return jax.shard_map(
        per_device, mesh=split, in_specs=in_specs, out_specs=P("tp", inst), check_vma=False
    )
```

```python
import jax
import jax.numpy as jnp
from jax import lax
from jax.experimental import pallas as pl
from jax.experimental.pallas import tpu as pltpu
from jax.sharding import Mesh, PartitionSpec as P

HD = 128
BLOCK = 128
MAXB = 4
SLOTS = 32
HEADS = 8
REQS = 8
PEERS = 64
MSG = 18
ROUTE_LIMIT = 60 * 1024 * 1024
very_low = -1e30
f32 = jnp.float32
bf16 = jnp.bfloat16

VMEM = pl.BlockSpec(memory_space=pltpu.VMEM)
HBM = pl.BlockSpec(memory_space=pltpu.HBM)
limit = pltpu.CompilerParams(vmem_limit_bytes=24 * 1024 * 1024)


def put_items(buf, items):
    for i in range(2):
        for j in range(HEADS + 1):
            buf[pl.ds(2 * j + i, PEERS, stride=MSG), :] = items[
                i * PEERS : (i + 1) * PEERS, j * HD : (j + 1) * HD
            ]


def get_items(buf):
    return jnp.concatenate(
        [
            jnp.concatenate(
                [buf[pl.ds(2 * j + i, PEERS, stride=MSG), :] for j in range(HEADS + 1)], axis=1
            )
            for i in range(2)
        ],
        axis=0,
    )


def route_kernel(table, ctx, q, out, where_to, buf):
    entries = REQS * MAXB
    row = lax.broadcasted_iota(jnp.int32, (entries, HD), 0)
    lane = lax.broadcasted_iota(jnp.int32, (entries, HD), 1)
    slot = jnp.concatenate(
        [jnp.broadcast_to(table[b : b + 1, :], (REQS, REQS)) for b in range(MAXB)], axis=0
    )
    length = jnp.broadcast_to(ctx[...], (entries, REQS))
    own = lane[:, :REQS] == (row[:, :REQS] & 7)
    slot = jnp.sum(jnp.where(own, slot, 0), axis=1, keepdims=True)
    length = jnp.sum(jnp.where(own, length, 0), axis=1, keepdims=True)
    slot = jnp.broadcast_to(slot, (entries, HD))
    count = jnp.clip(jnp.broadcast_to(length, (entries, HD)) - (row >> 3) * BLOCK, 0, BLOCK)
    holder = (slot >> 5).astype(f32)
    holders = jnp.sum(jnp.where(row == lane, holder, 0.0), axis=0, keepdims=True)
    earlier = jnp.where((holder == holders) & (lane < row), 1.0, 0.0)
    item = jnp.sum(earlier, axis=1, keepdims=True) * PEERS + holder
    pick = jnp.where(lane.astype(f32) == item, 1.0, 0.0).astype(bf16)
    where_to[...] = pick
    note = jnp.where(lane == 0, (slot & 31) + 1, jnp.where(lane == 1, count, 0)).astype(f32)
    side = jnp.concatenate([jnp.concatenate([q[...].astype(f32)] * MAXB, axis=0), note], axis=1)
    items = lax.dot_general(
        pick, side.astype(bf16), (((0,), (0,)), ((), ())), preferred_element_type=f32
    )
    put_items(buf, items)
    out[...] = buf[...].astype(bf16)


def attend_kernel(items, keys, values, out, buf, rows, counts):
    buf[...] = items[...].astype(f32)
    given = get_items(buf)
    queries, notes = given[:, : HEADS * HD], given[:, HEADS * HD :]
    slot_no = lax.broadcasted_iota(jnp.int32, (2 * PEERS, HD), 1).astype(f32) + 1.0
    pick = jnp.where(slot_no == notes[:, :1], 1.0, 0.0).astype(bf16)
    side = jnp.concatenate(
        [queries, jnp.broadcast_to(notes[:, 1:2], (2 * PEERS, HD))], axis=1
    ).astype(bf16)
    by_slot = lax.dot_general(
        pick, side, (((0,), (0,)), ((), ())), preferred_element_type=f32
    )[:SLOTS]
    for h in range(HEADS):
        rows[pl.ds(h, SLOTS, stride=HEADS), :] = by_slot[:, h * HD : (h + 1) * HD]
        counts[pl.ds(h, SLOTS, stride=HEADS), :] = by_slot[:, HEADS * HD :]
    parts = []
    for s in range(0, SLOTS, 2):
        pair = lax.dot_general(
            rows[s * 8 : s * 8 + 16, :].astype(bf16),
            keys[s : s + 2].reshape(2 * BLOCK, HD),
            (((1,), (1,)), ((), ())),
            preferred_element_type=f32,
        )
        parts += [pair[:8, :BLOCK], pair[8:, BLOCK:]]
    scores = jnp.concatenate(parts, axis=0) * HD ** (-0.5)
    token = lax.broadcasted_iota(jnp.int32, scores.shape, 1).astype(f32)
    usable = token < counts[...]
    scores = jnp.where(usable, scores, very_low)
    top = jnp.max(scores, axis=1, keepdims=True)
    weights = jnp.where(usable, jnp.exp(scores - top), 0.0)
    total = jnp.sum(weights, axis=1, keepdims=True)
    none = jnp.zeros((8, BLOCK), f32)
    parts = []
    for s in range(0, SLOTS, 2):
        first = jnp.concatenate([weights[s * 8 : s * 8 + 8], none], axis=1)
        second = jnp.concatenate([none, weights[s * 8 + 8 : s * 8 + 16]], axis=1)
        parts.append(
            jnp.dot(
                jnp.concatenate([first, second], axis=0).astype(bf16),
                values[s : s + 2].reshape(2 * BLOCK, HD),
                preferred_element_type=f32,
            )
        )
    alive = total > 0.0
    safe = jnp.where(alive, total, 1.0)
    rows[...] = jnp.concatenate(parts, axis=0) / safe
    lse = jnp.where(alive, top + jnp.log(safe), very_low)
    high = lse.astype(bf16).astype(f32)
    mid = (lse - high).astype(bf16).astype(f32)
    low = lse - high - mid
    lane = lax.broadcasted_iota(jnp.int32, (SLOTS * HEADS, HD), 1)
    head = lax.broadcasted_iota(jnp.int32, (SLOTS * HEADS, HD), 0) & 7
    note = jnp.where(
        lane == head,
        high,
        jnp.where(lane == head + 8, mid, jnp.where(lane == head + 16, low, 0.0)),
    )
    note = jnp.sum(note.reshape(SLOTS, HEADS, HD), axis=1)
    side = jnp.concatenate(
        [rows[pl.ds(h, SLOTS, stride=HEADS), :] for h in range(HEADS)] + [note], axis=1
    ).astype(bf16)
    back = jnp.dot(pick[:, :SLOTS], side, preferred_element_type=f32)
    put_items(buf, back)
    out[...] = buf[...].astype(bf16)


def merge_kernel(where_to, items, out, buf):
    buf[...] = items[...].astype(f32)
    by_entry = jnp.dot(where_to[...], get_items(buf).astype(bf16), preferred_element_type=f32)
    blocks = [by_entry[b * REQS : (b + 1) * REQS] for b in range(MAXB)]
    lses = []
    for block in blocks:
        note = block[:, HEADS * HD :]
        lses.append(note[:, :8] + note[:, 8:16] + note[:, 16:24])
    top = jnp.maximum(jnp.maximum(lses[0], lses[1]), jnp.maximum(lses[2], lses[3]))
    scales = [jnp.exp(v - top) for v in lses]
    total = scales[0] + scales[1] + scales[2] + scales[3]
    scales = [v / total for v in scales]
    whole = []
    for h in range(HEADS):
        at = slice(h * HD, (h + 1) * HD)
        whole.append(sum(v[:, h : h + 1] * block[:, at] for v, block in zip(scales, blocks)))
    whole = jnp.concatenate(whole, axis=1)
    out[...] = jnp.concatenate([whole] * 8, axis=0).astype(bf16)


def stage_kernel(*refs):
    n = (len(refs) - 1) // 2
    sources, targets, sems = refs[:n], refs[n : 2 * n], refs[-1]
    copies = []
    for a in range(n):
        step = sources[a].shape[0] // 4
        for k in range(4):
            part = pl.ds(k * step, step)
            copies.append(
                pltpu.make_async_copy(sources[a].at[part], targets[a].at[part], sems.at[a * 4 + k])
            )
    for copy in copies:
        copy.start()
    for copy in copies:
        copy.wait()


def stage(*arrays, name):
    return pl.pallas_call(
        stage_kernel,
        out_shape=tuple(jax.ShapeDtypeStruct(a.shape, a.dtype) for a in arrays),
        in_specs=[HBM] * len(arrays),
        out_specs=(VMEM,) * len(arrays),
        scratch_shapes=[pltpu.SemaphoreType.DMA((4 * len(arrays),))],
        compiler_params=limit,
        cost_estimate=pl.CostEstimate(flops=0, bytes_accessed=1 << 22, transcendentals=0),
        name=name,
    )(*arrays)


def project_kernel(attention, weight, out):
    left = attention[...]
    for n in range(8):
        part = jnp.dot(left, weight[n], preferred_element_type=f32)
        out[n * 64 : (n + 1) * 64, :] = part.astype(bf16)


def total_kernel(parts, out):
    got = parts[...].astype(f32).reshape(8, 8, 8, HD)
    out[...] = jnp.sum(got, axis=1).reshape(64, HD).astype(bf16)


def per_device(queries, pool_keys, pool_values, block_table, ctx_len, out_weight):
    inst = ("z", "x", "c")
    send, where_to = pl.pallas_call(
        route_kernel,
        out_shape=(
            jax.ShapeDtypeStruct((PEERS * MSG, HD), bf16),
            jax.ShapeDtypeStruct((REQS * MAXB, HD), bf16),
        ),
        in_specs=[VMEM, VMEM, VMEM],
        out_specs=(VMEM, VMEM),
        scratch_shapes=[pltpu.VMEM((PEERS * MSG, HD), f32)],
        compiler_params=pltpu.CompilerParams(vmem_limit_bytes=ROUTE_LIMIT),
        name="route",
    )(block_table.T, ctx_len[None, :], queries)
    out_weight, send = lax.optimization_barrier((out_weight, send))
    weights = lax.all_gather(out_weight, ("x", "c"), axis=0, tiled=False)
    items = lax.all_to_all(
        send.reshape(PEERS, HEADS + 1, 2, HD), inst, split_axis=0, concat_axis=0, tiled=True
    )
    keys, values = stage(pool_keys, pool_values, name="stage_blocks")
    back = pl.pallas_call(
        attend_kernel,
        out_shape=jax.ShapeDtypeStruct((PEERS * MSG, HD), bf16),
        in_specs=[VMEM, VMEM, VMEM],
        out_specs=VMEM,
        scratch_shapes=[
            pltpu.VMEM((PEERS * MSG, HD), f32),
            pltpu.VMEM((SLOTS * HEADS, HD), f32),
            pltpu.VMEM((SLOTS * HEADS, HD), f32),
        ],
        compiler_params=limit,
        name="attend",
    )(items.reshape(PEERS * MSG, HD), keys, values)
    partials = lax.all_to_all(
        back.reshape(PEERS, HEADS + 1, 2, HD), inst, split_axis=0, concat_axis=0, tiled=True
    )
    attention = pl.pallas_call(
        merge_kernel,
        out_shape=jax.ShapeDtypeStruct((8 * REQS, HEADS * HD), bf16),
        in_specs=[VMEM, VMEM],
        out_specs=VMEM,
        scratch_shapes=[pltpu.VMEM((PEERS * MSG, HD), f32)],
        compiler_params=limit,
        name="merge",
    )(where_to, partials.reshape(PEERS * MSG, HD))
    (weights,) = stage(weights, name="stage_weights")
    gathered = lax.all_to_all(
        attention.reshape(8, REQS, HEADS * HD), "z", split_axis=0, concat_axis=0, tiled=True
    )
    parts = pl.pallas_call(
        project_kernel,
        out_shape=jax.ShapeDtypeStruct((512, HD), bf16),
        in_specs=[VMEM, VMEM],
        out_specs=VMEM,
        compiler_params=limit,
        name="project",
    )(gathered.reshape(64, HEADS * HD), weights)
    swapped = lax.all_to_all(
        parts.reshape(64, 8, HD), ("x", "c", "tp"), split_axis=0, concat_axis=0, tiled=True
    )
    return pl.pallas_call(
        total_kernel,
        out_shape=jax.ShapeDtypeStruct((64, HD), bf16),
        in_specs=[VMEM],
        out_specs=VMEM,
        compiler_params=limit,
        name="total",
    )(swapped.reshape(512, HD))


def solution(mesh):
    split = Mesh(mesh.devices.reshape(8, 4, 2, 8), ("z", "x", "c", "tp"))
    inst = ("z", "x", "c")
    in_specs = (
        P(inst, "tp"),
        P(inst, None, "tp"),
        P(inst, None, "tp"),
        P(inst, None),
        P(inst),
        P("tp", inst),
    )
    return jax.shard_map(
        per_device, mesh=split, in_specs=in_specs, out_specs=P("tp", inst), check_vma=False
    )
```

```python
import jax
import jax.numpy as jnp
from jax import lax
from jax.experimental import pallas as pl
from jax.experimental.pallas import tpu as pltpu
from jax.sharding import Mesh, PartitionSpec as P

HD = 128
BLOCK = 128
MAXB = 4
SLOTS = 32
HEADS = 8
REQS = 8
PEERS = 64
MSG = 18
ROUTE_LIMIT = 60 * 1024 * 1024
very_low = -1e30
f32 = jnp.float32
bf16 = jnp.bfloat16

VMEM = pl.BlockSpec(memory_space=pltpu.VMEM)
HBM = pl.BlockSpec(memory_space=pltpu.HBM)
limit = pltpu.CompilerParams(vmem_limit_bytes=24 * 1024 * 1024)


def put_items(buf, items):
    for i in range(2):
        for j in range(HEADS + 1):
            buf[pl.ds(2 * j + i, PEERS, stride=MSG), :] = items[
                i * PEERS : (i + 1) * PEERS, j * HD : (j + 1) * HD
            ]


def get_items(buf):
    return jnp.concatenate(
        [
            jnp.concatenate(
                [buf[pl.ds(2 * j + i, PEERS, stride=MSG), :] for j in range(HEADS + 1)], axis=1
            )
            for i in range(2)
        ],
        axis=0,
    )


def route_kernel(table, ctx, q, out, where_to, buf):
    entries = REQS * MAXB
    row = lax.broadcasted_iota(jnp.int32, (entries, HD), 0)
    lane = lax.broadcasted_iota(jnp.int32, (entries, HD), 1)
    slot = jnp.concatenate(
        [jnp.broadcast_to(table[b : b + 1, :], (REQS, REQS)) for b in range(MAXB)], axis=0
    )
    length = jnp.broadcast_to(ctx[...], (entries, REQS))
    own = lane[:, :REQS] == (row[:, :REQS] & 7)
    slot = jnp.sum(jnp.where(own, slot, 0), axis=1, keepdims=True)
    length = jnp.sum(jnp.where(own, length, 0), axis=1, keepdims=True)
    slot = jnp.broadcast_to(slot, (entries, HD))
    count = jnp.clip(jnp.broadcast_to(length, (entries, HD)) - (row >> 3) * BLOCK, 0, BLOCK)
    holder = (slot >> 5).astype(f32)
    holders = jnp.sum(jnp.where(row == lane, holder, 0.0), axis=0, keepdims=True)
    earlier = jnp.where((holder == holders) & (lane < row), 1.0, 0.0)
    item = jnp.sum(earlier, axis=1, keepdims=True) * PEERS + holder
    pick = jnp.where(lane.astype(f32) == item, 1.0, 0.0).astype(bf16)
    where_to[...] = pick
    note = jnp.where(lane == 0, (slot & 31) + 1, jnp.where(lane == 1, count, 0)).astype(f32)
    side = jnp.concatenate([jnp.concatenate([q[...].astype(f32)] * MAXB, axis=0), note], axis=1)
    items = lax.dot_general(
        pick, side.astype(bf16), (((0,), (0,)), ((), ())), preferred_element_type=f32
    )
    put_items(buf, items)
    out[...] = buf[...].astype(bf16)


def attend_kernel(items, keys, values, out, buf, rows, counts):
    buf[...] = items[...].astype(f32)
    given = get_items(buf)
    queries, notes = given[:, : HEADS * HD], given[:, HEADS * HD :]
    slot_no = lax.broadcasted_iota(jnp.int32, (2 * PEERS, HD), 1).astype(f32) + 1.0
    pick = jnp.where(slot_no == notes[:, :1], 1.0, 0.0).astype(bf16)
    side = jnp.concatenate(
        [queries, jnp.broadcast_to(notes[:, 1:2], (2 * PEERS, HD))], axis=1
    ).astype(bf16)
    by_slot = lax.dot_general(
        pick, side, (((0,), (0,)), ((), ())), preferred_element_type=f32
    )[:SLOTS]
    for h in range(HEADS):
        rows[pl.ds(h, SLOTS, stride=HEADS), :] = by_slot[:, h * HD : (h + 1) * HD]
        counts[pl.ds(h, SLOTS, stride=HEADS), :] = by_slot[:, HEADS * HD :]
    parts = []
    for s in range(0, SLOTS, 2):
        pair = lax.dot_general(
            rows[s * 8 : s * 8 + 16, :].astype(bf16),
            keys[s : s + 2].reshape(2 * BLOCK, HD),
            (((1,), (1,)), ((), ())),
            preferred_element_type=f32,
        )
        parts += [pair[:8, :BLOCK], pair[8:, BLOCK:]]
    scores = jnp.concatenate(parts, axis=0) * HD ** (-0.5)
    token = lax.broadcasted_iota(jnp.int32, scores.shape, 1).astype(f32)
    usable = token < counts[...]
    scores = jnp.where(usable, scores, very_low)
    top = jnp.max(scores, axis=1, keepdims=True)
    weights = jnp.where(usable, jnp.exp(scores - top), 0.0)
    total = jnp.sum(weights, axis=1, keepdims=True)
    none = jnp.zeros((8, BLOCK), f32)
    parts = []
    for s in range(0, SLOTS, 2):
        first = jnp.concatenate([weights[s * 8 : s * 8 + 8], none], axis=1)
        second = jnp.concatenate([none, weights[s * 8 + 8 : s * 8 + 16]], axis=1)
        parts.append(
            jnp.dot(
                jnp.concatenate([first, second], axis=0).astype(bf16),
                values[s : s + 2].reshape(2 * BLOCK, HD),
                preferred_element_type=f32,
            )
        )
    alive = total > 0.0
    safe = jnp.where(alive, total, 1.0)
    rows[...] = jnp.concatenate(parts, axis=0) / safe
    lse = jnp.where(alive, top + jnp.log(safe), very_low)
    high = lse.astype(bf16).astype(f32)
    mid = (lse - high).astype(bf16).astype(f32)
    low = lse - high - mid
    lane = lax.broadcasted_iota(jnp.int32, (SLOTS * HEADS, HD), 1)
    head = lax.broadcasted_iota(jnp.int32, (SLOTS * HEADS, HD), 0) & 7
    note = jnp.where(
        lane == head,
        high,
        jnp.where(lane == head + 8, mid, jnp.where(lane == head + 16, low, 0.0)),
    )
    note = jnp.sum(note.reshape(SLOTS, HEADS, HD), axis=1)
    side = jnp.concatenate(
        [rows[pl.ds(h, SLOTS, stride=HEADS), :] for h in range(HEADS)] + [note], axis=1
    ).astype(bf16)
    back = jnp.dot(pick[:, :SLOTS], side, preferred_element_type=f32)
    put_items(buf, back)
    out[...] = buf[...].astype(bf16)


def merge_kernel(where_to, items, out, buf):
    buf[...] = items[...].astype(f32)
    by_entry = jnp.dot(where_to[...], get_items(buf).astype(bf16), preferred_element_type=f32)
    blocks = [by_entry[b * REQS : (b + 1) * REQS] for b in range(MAXB)]
    lses = []
    for block in blocks:
        note = block[:, HEADS * HD :]
        lses.append(note[:, :8] + note[:, 8:16] + note[:, 16:24])
    top = jnp.maximum(jnp.maximum(lses[0], lses[1]), jnp.maximum(lses[2], lses[3]))
    scales = [jnp.exp(v - top) for v in lses]
    total = scales[0] + scales[1] + scales[2] + scales[3]
    scales = [v / total for v in scales]
    whole = []
    for h in range(HEADS):
        at = slice(h * HD, (h + 1) * HD)
        whole.append(sum(v[:, h : h + 1] * block[:, at] for v, block in zip(scales, blocks)))
    whole = jnp.concatenate(whole, axis=1)
    out[...] = jnp.concatenate([whole] * 32, axis=0).astype(bf16)


def stage_kernel(*refs):
    n = (len(refs) - 1) // 2
    sources, targets, sems = refs[:n], refs[n : 2 * n], refs[-1]
    copies = []
    for a in range(n):
        step = sources[a].shape[0] // 4
        for k in range(4):
            part = pl.ds(k * step, step)
            copies.append(
                pltpu.make_async_copy(sources[a].at[part], targets[a].at[part], sems.at[a * 4 + k])
            )
    for copy in copies:
        copy.start()
    for copy in copies:
        copy.wait()


def stage(*arrays, name):
    return pl.pallas_call(
        stage_kernel,
        out_shape=tuple(jax.ShapeDtypeStruct(a.shape, a.dtype) for a in arrays),
        in_specs=[HBM] * len(arrays),
        out_specs=(VMEM,) * len(arrays),
        scratch_shapes=[pltpu.SemaphoreType.DMA((4 * len(arrays),))],
        compiler_params=limit,
        cost_estimate=pl.CostEstimate(flops=0, bytes_accessed=1 << 22, transcendentals=0),
        name=name,
    )(*arrays)


def project_kernel(attention, own, other, out):
    me = lax.axis_index("c")
    left = attention[...]
    for c, weight in ((me, own), (1 - me, other)):
        part = jnp.dot(left, weight[...], preferred_element_type=f32)
        out[pl.ds(pl.multiple_of(c * 256, 256), 256), :] = part.astype(bf16)


def total_kernel(parts, out):
    got = jnp.sum(parts[...].astype(f32).reshape(2, 8, 4, 8, HD), axis=1)
    out[...] = jnp.concatenate([got[c, x] for x in range(4) for c in range(2)]).astype(bf16)


def per_device(queries, pool_keys, pool_values, block_table, ctx_len, out_weight):
    inst = ("z", "x", "c")
    send, where_to = pl.pallas_call(
        route_kernel,
        out_shape=(
            jax.ShapeDtypeStruct((PEERS * MSG, HD), bf16),
            jax.ShapeDtypeStruct((REQS * MAXB, HD), bf16),
        ),
        in_specs=[VMEM, VMEM, VMEM],
        out_specs=(VMEM, VMEM),
        scratch_shapes=[pltpu.VMEM((PEERS * MSG, HD), f32)],
        compiler_params=pltpu.CompilerParams(vmem_limit_bytes=ROUTE_LIMIT),
        name="route",
    )(block_table.T, ctx_len[None, :], queries)
    items = lax.all_to_all(
        send.reshape(PEERS, HEADS + 1, 2, HD), inst, split_axis=0, concat_axis=0, tiled=True
    )
    keys, values = stage(pool_keys, pool_values, name="stage_blocks")
    out_weight, keys, values = lax.optimization_barrier((out_weight, keys, values))
    other_weight = lax.ppermute(out_weight, "c", [(0, 1), (1, 0)])
    items, other_weight = lax.optimization_barrier((items, other_weight))
    back = pl.pallas_call(
        attend_kernel,
        out_shape=jax.ShapeDtypeStruct((PEERS * MSG, HD), bf16),
        in_specs=[VMEM, VMEM, VMEM],
        out_specs=VMEM,
        scratch_shapes=[
            pltpu.VMEM((PEERS * MSG, HD), f32),
            pltpu.VMEM((SLOTS * HEADS, HD), f32),
            pltpu.VMEM((SLOTS * HEADS, HD), f32),
        ],
        compiler_params=limit,
        name="attend",
    )(items.reshape(PEERS * MSG, HD), keys, values)
    partials = lax.all_to_all(
        back.reshape(PEERS, HEADS + 1, 2, HD), inst, split_axis=0, concat_axis=0, tiled=True
    )
    attention = pl.pallas_call(
        merge_kernel,
        out_shape=jax.ShapeDtypeStruct((32 * REQS, HEADS * HD), bf16),
        in_specs=[VMEM, VMEM],
        out_specs=VMEM,
        scratch_shapes=[pltpu.VMEM((PEERS * MSG, HD), f32)],
        compiler_params=limit,
        name="merge",
    )(where_to, partials.reshape(PEERS * MSG, HD))
    gathered = lax.all_to_all(
        attention.reshape(32, REQS, HEADS * HD), ("z", "x"), split_axis=0, concat_axis=0, tiled=True
    )
    parts = pl.pallas_call(
        project_kernel,
        out_shape=jax.ShapeDtypeStruct((512, HD), bf16),
        in_specs=[VMEM] * 3,
        out_specs=VMEM,
        compiler_params=limit,
        name="project",
    )(gathered.reshape(256, HEADS * HD), out_weight, other_weight)
    swapped = lax.all_to_all(
        parts.reshape(16, 32, HD), ("c", "tp"), split_axis=0, concat_axis=0, tiled=True
    )
    return pl.pallas_call(
        total_kernel,
        out_shape=jax.ShapeDtypeStruct((64, HD), bf16),
        in_specs=[VMEM],
        out_specs=VMEM,
        compiler_params=limit,
        name="total",
    )(swapped.reshape(512, HD))


def solution(mesh):
    split = Mesh(mesh.devices.reshape(8, 4, 2, 8), ("z", "x", "c", "tp"))
    inst = ("z", "x", "c")
    in_specs = (
        P(inst, "tp"),
        P(inst, None, "tp"),
        P(inst, None, "tp"),
        P(inst, None),
        P(inst),
        P("tp", inst),
    )
    return jax.shard_map(
        per_device, mesh=split, in_specs=in_specs, out_specs=P("tp", inst), check_vma=False
    )
```

```python
import jax
import jax.numpy as jnp
from jax import lax
from jax.experimental import pallas as pl
from jax.experimental.pallas import tpu as pltpu
from jax.sharding import Mesh, PartitionSpec as P

HD = 128
BLOCK = 128
MAXB = 4
SLOTS = 32
HEADS = 8
REQS = 8
PEERS = 64
MSG = 18
ROUTE_LIMIT = 60 * 1024 * 1024
very_low = -1e30
f32 = jnp.float32
bf16 = jnp.bfloat16

VMEM = pl.BlockSpec(memory_space=pltpu.VMEM)
HBM = pl.BlockSpec(memory_space=pltpu.HBM)
limit = pltpu.CompilerParams(vmem_limit_bytes=24 * 1024 * 1024)


def put_items(buf, items):
    for i in range(2):
        for j in range(HEADS + 1):
            buf[pl.ds(2 * j + i, PEERS, stride=MSG), :] = items[
                i * PEERS : (i + 1) * PEERS, j * HD : (j + 1) * HD
            ]


def get_items(buf):
    return jnp.concatenate(
        [
            jnp.concatenate(
                [buf[pl.ds(2 * j + i, PEERS, stride=MSG), :] for j in range(HEADS + 1)], axis=1
            )
            for i in range(2)
        ],
        axis=0,
    )


def route_kernel(table, ctx, q, out, where_to, buf):
    entries = REQS * MAXB
    row = lax.broadcasted_iota(jnp.int32, (entries, HD), 0)
    lane = lax.broadcasted_iota(jnp.int32, (entries, HD), 1)
    slot = jnp.concatenate(
        [jnp.broadcast_to(table[b : b + 1, :], (REQS, REQS)) for b in range(MAXB)], axis=0
    )
    length = jnp.broadcast_to(ctx[...], (entries, REQS))
    own = lane[:, :REQS] == (row[:, :REQS] & 7)
    slot = jnp.sum(jnp.where(own, slot, 0), axis=1, keepdims=True)
    length = jnp.sum(jnp.where(own, length, 0), axis=1, keepdims=True)
    slot = jnp.broadcast_to(slot, (entries, HD))
    count = jnp.clip(jnp.broadcast_to(length, (entries, HD)) - (row >> 3) * BLOCK, 0, BLOCK)
    inst = slot >> 5
    holder = ((inst & 1) * 32 + (inst >> 3) * 4 + ((inst >> 1) & 3)).astype(f32)
    holders = jnp.sum(jnp.where(row == lane, holder, 0.0), axis=0, keepdims=True)
    earlier = jnp.where((holder == holders) & (lane < row), 1.0, 0.0)
    item = jnp.sum(earlier, axis=1, keepdims=True) * PEERS + holder
    pick = jnp.where(lane.astype(f32) == item, 1.0, 0.0).astype(bf16)
    where_to[...] = pick
    note = jnp.where(lane == 0, (slot & 31) + 1, jnp.where(lane == 1, count, 0)).astype(f32)
    side = jnp.concatenate([jnp.concatenate([q[...].astype(f32)] * MAXB, axis=0), note], axis=1)
    items = lax.dot_general(
        pick, side.astype(bf16), (((0,), (0,)), ((), ())), preferred_element_type=f32
    )
    put_items(buf, items)
    out[...] = buf[...].astype(bf16)


def attend_kernel(items, keys, values, out, buf, rows, counts):
    buf[...] = items[...].astype(f32)
    given = get_items(buf)
    queries, notes = given[:, : HEADS * HD], given[:, HEADS * HD :]
    slot_no = lax.broadcasted_iota(jnp.int32, (2 * PEERS, HD), 1).astype(f32) + 1.0
    pick = jnp.where(slot_no == notes[:, :1], 1.0, 0.0).astype(bf16)
    side = jnp.concatenate(
        [queries, jnp.broadcast_to(notes[:, 1:2], (2 * PEERS, HD))], axis=1
    ).astype(bf16)
    by_slot = lax.dot_general(
        pick, side, (((0,), (0,)), ((), ())), preferred_element_type=f32
    )[:SLOTS]
    for h in range(HEADS):
        rows[pl.ds(h, SLOTS, stride=HEADS), :] = by_slot[:, h * HD : (h + 1) * HD]
        counts[pl.ds(h, SLOTS, stride=HEADS), :] = by_slot[:, HEADS * HD :]
    parts = []
    for s in range(0, SLOTS, 2):
        pair = lax.dot_general(
            rows[s * 8 : s * 8 + 16, :].astype(bf16),
            keys[s : s + 2].reshape(2 * BLOCK, HD),
            (((1,), (1,)), ((), ())),
            preferred_element_type=f32,
        )
        parts += [pair[:8, :BLOCK], pair[8:, BLOCK:]]
    scores = jnp.concatenate(parts, axis=0) * HD ** (-0.5)
    token = lax.broadcasted_iota(jnp.int32, scores.shape, 1).astype(f32)
    usable = token < counts[...]
    scores = jnp.where(usable, scores, very_low)
    top = jnp.max(scores, axis=1, keepdims=True)
    weights = jnp.where(usable, jnp.exp(scores - top), 0.0)
    total = jnp.sum(weights, axis=1, keepdims=True)
    none = jnp.zeros((8, BLOCK), f32)
    parts = []
    for s in range(0, SLOTS, 2):
        first = jnp.concatenate([weights[s * 8 : s * 8 + 8], none], axis=1)
        second = jnp.concatenate([none, weights[s * 8 + 8 : s * 8 + 16]], axis=1)
        parts.append(
            jnp.dot(
                jnp.concatenate([first, second], axis=0).astype(bf16),
                values[s : s + 2].reshape(2 * BLOCK, HD),
                preferred_element_type=f32,
            )
        )
    alive = total > 0.0
    safe = jnp.where(alive, total, 1.0)
    rows[...] = jnp.concatenate(parts, axis=0) / safe
    lse = jnp.where(alive, top + jnp.log(safe), very_low)
    high = lse.astype(bf16).astype(f32)
    mid = (lse - high).astype(bf16).astype(f32)
    low = lse - high - mid
    lane = lax.broadcasted_iota(jnp.int32, (SLOTS * HEADS, HD), 1)
    head = lax.broadcasted_iota(jnp.int32, (SLOTS * HEADS, HD), 0) & 7
    note = jnp.where(
        lane == head,
        high,
        jnp.where(lane == head + 8, mid, jnp.where(lane == head + 16, low, 0.0)),
    )
    note = jnp.sum(note.reshape(SLOTS, HEADS, HD), axis=1)
    side = jnp.concatenate(
        [rows[pl.ds(h, SLOTS, stride=HEADS), :] for h in range(HEADS)] + [note], axis=1
    ).astype(bf16)
    back = jnp.dot(pick[:, :SLOTS], side, preferred_element_type=f32)
    put_items(buf, back)
    out[...] = buf[...].astype(bf16)


def merge_kernel(where_to, items, out, buf):
    buf[...] = items[...].astype(f32)
    by_entry = jnp.dot(where_to[...], get_items(buf).astype(bf16), preferred_element_type=f32)
    blocks = [by_entry[b * REQS : (b + 1) * REQS] for b in range(MAXB)]
    lses = []
    for block in blocks:
        note = block[:, HEADS * HD :]
        lses.append(note[:, :8] + note[:, 8:16] + note[:, 16:24])
    top = jnp.maximum(jnp.maximum(lses[0], lses[1]), jnp.maximum(lses[2], lses[3]))
    scales = [jnp.exp(v - top) for v in lses]
    total = scales[0] + scales[1] + scales[2] + scales[3]
    scales = [v / total for v in scales]
    whole = []
    for h in range(HEADS):
        at = slice(h * HD, (h + 1) * HD)
        whole.append(sum(v[:, h : h + 1] * block[:, at] for v, block in zip(scales, blocks)))
    whole = jnp.concatenate(whole, axis=1)
    out[...] = jnp.concatenate([whole] * 32, axis=0).astype(bf16)


def stage_kernel(*refs):
    n = (len(refs) - 1) // 2
    sources, targets, sems = refs[:n], refs[n : 2 * n], refs[-1]
    copies = []
    for a in range(n):
        step = sources[a].shape[0] // 4
        for k in range(4):
            part = pl.ds(k * step, step)
            copies.append(
                pltpu.make_async_copy(sources[a].at[part], targets[a].at[part], sems.at[a * 4 + k])
            )
    for copy in copies:
        copy.start()
    for copy in copies:
        copy.wait()


def stage(*arrays, name):
    return pl.pallas_call(
        stage_kernel,
        out_shape=tuple(jax.ShapeDtypeStruct(a.shape, a.dtype) for a in arrays),
        in_specs=[HBM] * len(arrays),
        out_specs=(VMEM,) * len(arrays),
        scratch_shapes=[pltpu.SemaphoreType.DMA((4 * len(arrays),))],
        compiler_params=limit,
        cost_estimate=pl.CostEstimate(flops=0, bytes_accessed=1 << 22, transcendentals=0),
        name=name,
    )(*arrays)


def project_kernel(attention, own, other, out):
    me = lax.axis_index("c")
    left = attention[...]
    for c, weight in ((me, own), (1 - me, other)):
        part = jnp.dot(left, weight[...], preferred_element_type=f32)
        part = part.reshape(4, 8, 8, HD)
        part = jnp.concatenate([part[x, z] for z in range(8) for x in range(4)])
        out[pl.ds(pl.multiple_of(c * 256, 256), 256), :] = part.astype(bf16)


def total_kernel(parts, out):
    got = jnp.sum(parts[...].astype(f32).reshape(2, 8, 4, 8, HD), axis=1)
    out[...] = jnp.concatenate([got[c, x] for x in range(4) for c in range(2)]).astype(bf16)


def per_device(queries, pool_keys, pool_values, block_table, ctx_len, out_weight):
    inst = ("c", "z", "x")
    send, where_to = pl.pallas_call(
        route_kernel,
        out_shape=(
            jax.ShapeDtypeStruct((PEERS * MSG, HD), bf16),
            jax.ShapeDtypeStruct((REQS * MAXB, HD), bf16),
        ),
        in_specs=[VMEM, VMEM, VMEM],
        out_specs=(VMEM, VMEM),
        scratch_shapes=[pltpu.VMEM((PEERS * MSG, HD), f32)],
        compiler_params=pltpu.CompilerParams(vmem_limit_bytes=ROUTE_LIMIT),
        name="route",
    )(block_table.T, ctx_len[None, :], queries)
    items = lax.all_to_all(
        send.reshape(PEERS, HEADS + 1, 2, HD), inst, split_axis=0, concat_axis=0, tiled=True
    )
    keys, values = stage(pool_keys, pool_values, name="stage_blocks")
    out_weight, keys, values = lax.optimization_barrier((out_weight, keys, values))
    other_weight = lax.ppermute(out_weight, "c", [(0, 1), (1, 0)])
    items, other_weight = lax.optimization_barrier((items, other_weight))
    back = pl.pallas_call(
        attend_kernel,
        out_shape=jax.ShapeDtypeStruct((PEERS * MSG, HD), bf16),
        in_specs=[VMEM, VMEM, VMEM],
        out_specs=VMEM,
        scratch_shapes=[
            pltpu.VMEM((PEERS * MSG, HD), f32),
            pltpu.VMEM((SLOTS * HEADS, HD), f32),
            pltpu.VMEM((SLOTS * HEADS, HD), f32),
        ],
        compiler_params=limit,
        name="attend",
    )(items.reshape(PEERS * MSG, HD), keys, values)
    partials = lax.all_to_all(
        back.reshape(PEERS, HEADS + 1, 2, HD), inst, split_axis=0, concat_axis=0, tiled=True
    )
    attention = pl.pallas_call(
        merge_kernel,
        out_shape=jax.ShapeDtypeStruct((32 * REQS, HEADS * HD), bf16),
        in_specs=[VMEM, VMEM],
        out_specs=VMEM,
        scratch_shapes=[pltpu.VMEM((PEERS * MSG, HD), f32)],
        compiler_params=limit,
        name="merge",
    )(where_to, partials.reshape(PEERS * MSG, HD))
    gathered = lax.all_to_all(
        attention.reshape(32, REQS, HEADS * HD), ("x", "z"), split_axis=0, concat_axis=0, tiled=True
    )
    parts = pl.pallas_call(
        project_kernel,
        out_shape=jax.ShapeDtypeStruct((512, HD), bf16),
        in_specs=[VMEM] * 3,
        out_specs=VMEM,
        compiler_params=limit,
        name="project",
    )(gathered.reshape(256, HEADS * HD), out_weight, other_weight)
    swapped = lax.all_to_all(
        parts.reshape(16, 32, HD), ("c", "tp"), split_axis=0, concat_axis=0, tiled=True
    )
    return pl.pallas_call(
        total_kernel,
        out_shape=jax.ShapeDtypeStruct((64, HD), bf16),
        in_specs=[VMEM],
        out_specs=VMEM,
        compiler_params=limit,
        name="total",
    )(swapped.reshape(512, HD))


def solution(mesh):
    split = Mesh(mesh.devices.reshape(8, 4, 2, 8), ("z", "x", "c", "tp"))
    inst = ("z", "x", "c")
    in_specs = (
        P(inst, "tp"),
        P(inst, None, "tp"),
        P(inst, None, "tp"),
        P(inst, None),
        P(inst),
        P("tp", inst),
    )
    return jax.shard_map(
        per_device, mesh=split, in_specs=in_specs, out_specs=P("tp", inst), check_vma=False
    )
```

```python
import jax
import jax.numpy as jnp
from jax import lax
from jax.experimental import pallas as pl
from jax.experimental.pallas import tpu as pltpu
from jax.sharding import Mesh, PartitionSpec as P

HD = 128
BLOCK = 128
MAXB = 4
SLOTS = 32
HEADS = 8
REQS = 8
PEERS = 64
MSG = 18
ROWS = PEERS * MSG
ROUTE_LIMIT = 60 * 1024 * 1024
very_low = -1e30
f32 = jnp.float32
bf16 = jnp.bfloat16

VMEM = pl.BlockSpec(memory_space=pltpu.VMEM)
HBM = pl.BlockSpec(memory_space=pltpu.HBM)
limit = pltpu.CompilerParams(vmem_limit_bytes=24 * 1024 * 1024)


def put_items(buf, items):
    for i in range(2):
        for j in range(HEADS + 1):
            buf[pl.ds(2 * j + i, PEERS, stride=MSG), :] = items[
                i * PEERS : (i + 1) * PEERS, j * HD : (j + 1) * HD
            ]


def get_items(buf):
    return jnp.concatenate(
        [
            jnp.concatenate(
                [buf[pl.ds(2 * j + i, PEERS, stride=MSG), :] for j in range(HEADS + 1)], axis=1
            )
            for i in range(2)
        ],
        axis=0,
    )


def route_kernel(table, ctx, q, out, where_to, buf):
    entries = REQS * MAXB
    row = lax.broadcasted_iota(jnp.int32, (entries, HD), 0)
    lane = lax.broadcasted_iota(jnp.int32, (entries, HD), 1)
    slot = jnp.concatenate(
        [jnp.broadcast_to(table[b : b + 1, :], (REQS, REQS)) for b in range(MAXB)], axis=0
    )
    length = jnp.broadcast_to(ctx[...], (entries, REQS))
    own = lane[:, :REQS] == (row[:, :REQS] & 7)
    slot = jnp.sum(jnp.where(own, slot, 0), axis=1, keepdims=True)
    length = jnp.sum(jnp.where(own, length, 0), axis=1, keepdims=True)
    slot = jnp.broadcast_to(slot, (entries, HD))
    count = jnp.clip(jnp.broadcast_to(length, (entries, HD)) - (row >> 3) * BLOCK, 0, BLOCK)
    inst = slot >> 5
    holder = ((inst & 1) * 32 + (inst >> 3) * 4 + ((inst >> 1) & 3)).astype(f32)
    holders = jnp.sum(jnp.where(row == lane, holder, 0.0), axis=0, keepdims=True)
    earlier = jnp.where((holder == holders) & (lane < row), 1.0, 0.0)
    item = jnp.sum(earlier, axis=1, keepdims=True) * PEERS + holder
    pick = jnp.where(lane.astype(f32) == item, 1.0, 0.0).astype(bf16)
    where_to[...] = pick
    note = jnp.where(lane == 0, (slot & 31) + 1, jnp.where(lane == 1, count, 0)).astype(f32)
    side = jnp.concatenate([jnp.concatenate([q[...].astype(f32)] * MAXB, axis=0), note], axis=1)
    items = lax.dot_general(
        pick, side.astype(bf16), (((0,), (0,)), ((), ())), preferred_element_type=f32
    )
    put_items(buf, items)
    out[...] = buf[:ROWS, :].astype(bf16)


def attend_kernel(items, keys, values, out, buf, rows, counts):
    buf[:ROWS, :] = items[...].astype(f32)
    given = get_items(buf)
    queries, notes = given[:, : HEADS * HD], given[:, HEADS * HD :]
    slot_no = lax.broadcasted_iota(jnp.int32, (2 * PEERS, HD), 1).astype(f32) + 1.0
    pick = jnp.where(slot_no == notes[:, :1], 1.0, 0.0).astype(bf16)
    side = jnp.concatenate(
        [queries, jnp.broadcast_to(notes[:, 1:2], (2 * PEERS, HD))], axis=1
    ).astype(bf16)
    by_slot = lax.dot_general(
        pick[:, :SLOTS], side, (((0,), (0,)), ((), ())), preferred_element_type=f32
    )
    for h in range(HEADS):
        rows[pl.ds(h, SLOTS, stride=HEADS), :] = by_slot[:, h * HD : (h + 1) * HD]
        counts[pl.ds(h, SLOTS, stride=HEADS), :] = by_slot[:, HEADS * HD :]
    parts = []
    for s in range(0, SLOTS, 2):
        pair = lax.dot_general(
            rows[s * 8 : s * 8 + 16, :].astype(bf16),
            keys[s : s + 2].reshape(2 * BLOCK, HD),
            (((1,), (1,)), ((), ())),
            preferred_element_type=f32,
        )
        parts += [pair[:8, :BLOCK], pair[8:, BLOCK:]]
    scores = jnp.concatenate(parts, axis=0) * HD ** (-0.5)
    token = lax.broadcasted_iota(jnp.int32, scores.shape, 1).astype(f32)
    usable = token < counts[: SLOTS * HEADS, :]
    scores = jnp.where(usable, scores, very_low)
    top = jnp.max(scores, axis=1, keepdims=True)
    weights = jnp.where(usable, jnp.exp(scores - top), 0.0)
    total = jnp.sum(weights, axis=1, keepdims=True)
    none = jnp.zeros((8, BLOCK), f32)
    parts = []
    for s in range(0, SLOTS, 2):
        first = jnp.concatenate([weights[s * 8 : s * 8 + 8], none], axis=1)
        second = jnp.concatenate([none, weights[s * 8 + 8 : s * 8 + 16]], axis=1)
        parts.append(
            jnp.dot(
                jnp.concatenate([first, second], axis=0).astype(bf16),
                values[s : s + 2].reshape(2 * BLOCK, HD),
                preferred_element_type=f32,
            )
        )
    alive = total > 0.0
    safe = jnp.where(alive, total, 1.0)
    rows[: SLOTS * HEADS, :] = jnp.concatenate(parts, axis=0) / safe
    lse = jnp.where(alive, top + jnp.log(safe), very_low)
    high = lse.astype(bf16).astype(f32)
    mid = (lse - high).astype(bf16).astype(f32)
    low = lse - high - mid
    lane = lax.broadcasted_iota(jnp.int32, (SLOTS * HEADS, HD), 1)
    head = lax.broadcasted_iota(jnp.int32, (SLOTS * HEADS, HD), 0) & 7
    note = jnp.where(
        lane == head,
        high,
        jnp.where(lane == head + 8, mid, jnp.where(lane == head + 16, low, 0.0)),
    )
    note = jnp.sum(note.reshape(SLOTS, HEADS, HD), axis=1)
    side = jnp.concatenate(
        [rows[pl.ds(h, SLOTS, stride=HEADS), :] for h in range(HEADS)] + [note], axis=1
    ).astype(bf16)
    back = jnp.dot(pick[:, :SLOTS], side, preferred_element_type=f32)
    put_items(buf, back)
    out[...] = buf[:ROWS, :].astype(bf16)


def merge_kernel(where_to, items, out, buf):
    buf[:ROWS, :] = items[...].astype(f32)
    by_entry = jnp.dot(where_to[...], get_items(buf).astype(bf16), preferred_element_type=f32)
    blocks = [by_entry[b * REQS : (b + 1) * REQS] for b in range(MAXB)]
    lses = []
    for block in blocks:
        note = block[:, HEADS * HD :]
        lses.append(note[:, :8] + note[:, 8:16] + note[:, 16:24])
    top = jnp.maximum(jnp.maximum(lses[0], lses[1]), jnp.maximum(lses[2], lses[3]))
    scales = [jnp.exp(v - top) for v in lses]
    total = scales[0] + scales[1] + scales[2] + scales[3]
    scales = [v / total for v in scales]
    whole = []
    for h in range(HEADS):
        at = slice(h * HD, (h + 1) * HD)
        whole.append(sum(v[:, h : h + 1] * block[:, at] for v, block in zip(scales, blocks)))
    whole = jnp.concatenate(whole, axis=1)
    out[...] = jnp.concatenate([whole] * 32, axis=0).astype(bf16)


def stage_kernel(*refs):
    n = (len(refs) - 1) // 2
    sources, targets, sems = refs[:n], refs[n : 2 * n], refs[-1]
    copies = []
    for a in range(n):
        step = sources[a].shape[0] // 4
        for k in range(4):
            part = pl.ds(k * step, step)
            copies.append(
                pltpu.make_async_copy(sources[a].at[part], targets[a].at[part], sems.at[a * 4 + k])
            )
    for copy in copies:
        copy.start()
    for copy in copies:
        copy.wait()


def stage(*arrays, name):
    return pl.pallas_call(
        stage_kernel,
        out_shape=tuple(jax.ShapeDtypeStruct(a.shape, a.dtype) for a in arrays),
        in_specs=[HBM] * len(arrays),
        out_specs=(VMEM,) * len(arrays),
        scratch_shapes=[pltpu.SemaphoreType.DMA((4 * len(arrays),))],
        compiler_params=limit,
        cost_estimate=pl.CostEstimate(flops=0, bytes_accessed=1 << 22, transcendentals=0),
        name=name,
    )(*arrays)


def project_kernel(attention, own, other, out):
    me = lax.axis_index("c")
    left = attention[...]
    for c, weight in ((me, own), (1 - me, other)):
        part = jnp.dot(left, weight[...], preferred_element_type=f32)
        part = part.reshape(4, 8, 8, HD)
        part = jnp.concatenate([part[x, z] for z in range(8) for x in range(4)])
        out[pl.ds(pl.multiple_of(c * 256, 256), 256), :] = part.astype(bf16)


def total_kernel(parts, out):
    got = jnp.sum(parts[...].astype(f32).reshape(2, 8, 4, 8, HD), axis=1)
    out[...] = jnp.concatenate([got[c, x] for x in range(4) for c in range(2)]).astype(bf16)


def per_device(queries, pool_keys, pool_values, block_table, ctx_len, out_weight):
    inst = ("c", "z", "x")
    send, where_to = pl.pallas_call(
        route_kernel,
        out_shape=(
            jax.ShapeDtypeStruct((ROWS, HD), bf16),
            jax.ShapeDtypeStruct((REQS * MAXB, HD), bf16),
        ),
        in_specs=[VMEM, VMEM, VMEM],
        out_specs=(VMEM, VMEM),
        scratch_shapes=[pltpu.VMEM((ROWS + 32, HD), f32)],
        compiler_params=pltpu.CompilerParams(vmem_limit_bytes=ROUTE_LIMIT),
        name="route",
    )(block_table.T, ctx_len[None, :], queries)
    items = lax.all_to_all(
        send.reshape(PEERS, HEADS + 1, 2, HD), inst, split_axis=0, concat_axis=0, tiled=True
    )
    keys, values = stage(pool_keys, pool_values, name="stage_blocks")
    out_weight, keys, values = lax.optimization_barrier((out_weight, keys, values))
    other_weight = lax.ppermute(out_weight, "c", [(0, 1), (1, 0)])
    items, other_weight = lax.optimization_barrier((items, other_weight))
    back = pl.pallas_call(
        attend_kernel,
        out_shape=jax.ShapeDtypeStruct((ROWS, HD), bf16),
        in_specs=[VMEM, VMEM, VMEM],
        out_specs=VMEM,
        scratch_shapes=[
            pltpu.VMEM((ROWS + 32, HD), f32),
            pltpu.VMEM((SLOTS * HEADS + 16, HD), f32),
            pltpu.VMEM((SLOTS * HEADS + 16, HD), f32),
        ],
        compiler_params=limit,
        name="attend",
    )(items.reshape(ROWS, HD), keys, values)
    partials = lax.all_to_all(
        back.reshape(PEERS, HEADS + 1, 2, HD), inst, split_axis=0, concat_axis=0, tiled=True
    )
    attention = pl.pallas_call(
        merge_kernel,
        out_shape=jax.ShapeDtypeStruct((32 * REQS, HEADS * HD), bf16),
        in_specs=[VMEM, VMEM],
        out_specs=VMEM,
        scratch_shapes=[pltpu.VMEM((ROWS + 32, HD), f32)],
        compiler_params=limit,
        name="merge",
    )(where_to, partials.reshape(ROWS, HD))
    gathered = lax.all_to_all(
        attention.reshape(32, REQS, HEADS * HD), ("x", "z"), split_axis=0, concat_axis=0, tiled=True
    )
    parts = pl.pallas_call(
        project_kernel,
        out_shape=jax.ShapeDtypeStruct((512, HD), bf16),
        in_specs=[VMEM] * 3,
        out_specs=VMEM,
        compiler_params=limit,
        name="project",
    )(gathered.reshape(256, HEADS * HD), out_weight, other_weight)
    swapped = lax.all_to_all(
        parts.reshape(16, 32, HD), ("c", "tp"), split_axis=0, concat_axis=0, tiled=True
    )
    return pl.pallas_call(
        total_kernel,
        out_shape=jax.ShapeDtypeStruct((64, HD), bf16),
        in_specs=[VMEM],
        out_specs=VMEM,
        compiler_params=limit,
        name="total",
    )(swapped.reshape(512, HD))


def solution(mesh):
    split = Mesh(mesh.devices.reshape(8, 4, 2, 8), ("z", "x", "c", "tp"))
    inst = ("z", "x", "c")
    in_specs = (
        P(inst, "tp"),
        P(inst, None, "tp"),
        P(inst, None, "tp"),
        P(inst, None),
        P(inst),
        P("tp", inst),
    )
    return jax.shard_map(
        per_device, mesh=split, in_specs=in_specs, out_specs=P("tp", inst), check_vma=False
    )
```

```python
import jax
import jax.numpy as jnp
from jax import lax
from jax.experimental import pallas as pl
from jax.experimental.pallas import tpu as pltpu
from jax.sharding import Mesh, PartitionSpec as P

HD = 128
BLOCK = 128
MAXB = 4
SLOTS = 64
HEADS = 8
REQS = 8
PEERS = 32
PER = 4
MSG = 9 * PER
ROWS = PEERS * MSG
ROUTE_LIMIT = 60 * 1024 * 1024
very_low = -1e30
f32 = jnp.float32
bf16 = jnp.bfloat16

VMEM = pl.BlockSpec(memory_space=pltpu.VMEM)
HBM = pl.BlockSpec(memory_space=pltpu.HBM)
limit = pltpu.CompilerParams(vmem_limit_bytes=16 * 1024 * 1024)


def put_items(buf, items):
    for i in range(PER):
        for j in range(HEADS + 1):
            buf[pl.ds(PER * j + i, PEERS, stride=MSG), :] = items[
                i * PEERS : (i + 1) * PEERS, j * HD : (j + 1) * HD
            ]


def get_items(buf):
    return jnp.concatenate(
        [
            jnp.concatenate(
                [buf[pl.ds(PER * j + i, PEERS, stride=MSG), :] for j in range(HEADS + 1)], axis=1
            )
            for i in range(PER)
        ],
        axis=0,
    )


def route_kernel(table, ctx, q, out, where_to, buf):
    entries = REQS * MAXB
    row = lax.broadcasted_iota(jnp.int32, (entries, HD), 0)
    lane = lax.broadcasted_iota(jnp.int32, (entries, HD), 1)
    slot = jnp.concatenate(
        [jnp.broadcast_to(table[b : b + 1, :], (REQS, REQS)) for b in range(MAXB)], axis=0
    )
    length = jnp.broadcast_to(ctx[...], (entries, REQS))
    own = lane[:, :REQS] == (row[:, :REQS] & 7)
    slot = jnp.sum(jnp.where(own, slot, 0), axis=1, keepdims=True)
    length = jnp.sum(jnp.where(own, length, 0), axis=1, keepdims=True)
    slot = jnp.broadcast_to(slot, (entries, HD))
    count = jnp.clip(jnp.broadcast_to(length, (entries, HD)) - (row >> 3) * BLOCK, 0, BLOCK)
    inst = slot >> 5
    holder = inst.astype(f32)
    holders = jnp.sum(jnp.where(row == lane, holder, 0.0), axis=0, keepdims=True)
    earlier = jnp.where((holder == holders) & (lane < row), 1.0, 0.0)
    away = (inst & 1) ^ lax.axis_index("c")
    place = (away * 2 * PEERS + (inst >> 1)).astype(f32)
    item = jnp.sum(earlier, axis=1, keepdims=True) * PEERS + place
    pick = jnp.where(lane.astype(f32) == item, 1.0, 0.0).astype(bf16)
    where_to[...] = pick
    note = jnp.where(lane == 0, away * 32 + (slot & 31) + 1, jnp.where(lane == 1, count, 0)).astype(f32)
    side = jnp.concatenate([jnp.concatenate([q[...].astype(f32)] * MAXB, axis=0), note], axis=1)
    items = lax.dot_general(
        pick, side.astype(bf16), (((0,), (0,)), ((), ())), preferred_element_type=f32
    )
    put_items(buf, items)
    out[...] = buf[:ROWS, :].astype(bf16)


def unpack_kernel(items, picks, slots, buf):
    buf[:ROWS, :] = items[...].astype(f32)
    given = get_items(buf)
    queries, notes = given[:, : HEADS * HD], given[:, HEADS * HD :]
    slot_no = lax.broadcasted_iota(jnp.int32, (PER * PEERS, HD), 1).astype(f32) + 1.0
    pick = jnp.where(slot_no == notes[:, :1], 1.0, 0.0).astype(bf16)
    side = jnp.concatenate(
        [queries, jnp.broadcast_to(notes[:, 1:2], (PER * PEERS, HD))], axis=1
    ).astype(bf16)
    by_slot = lax.dot_general(
        pick[:, :SLOTS], side, (((0,), (0,)), ((), ())), preferred_element_type=f32
    )
    picks[...] = pick
    slots[...] = by_slot


def attend_kernel(pick, by_slot, keys, values, other_keys, other_values, out, buf, rows, counts):
    for h in range(HEADS):
        rows[pl.ds(h, SLOTS, stride=HEADS), :] = by_slot[:, h * HD : (h + 1) * HD]
        counts[pl.ds(h, SLOTS, stride=HEADS), :] = by_slot[:, HEADS * HD :]
    parts = []
    for s in range(0, SLOTS, 2):
        pair = lax.dot_general(
            rows[s * 8 : s * 8 + 16, :].astype(bf16),
            (keys if s < 32 else other_keys)[s % 32 : s % 32 + 2].reshape(2 * BLOCK, HD),
            (((1,), (1,)), ((), ())),
            preferred_element_type=f32,
        )
        parts += [pair[:8, :BLOCK], pair[8:, BLOCK:]]
    scores = jnp.concatenate(parts, axis=0) * HD ** (-0.5)
    token = lax.broadcasted_iota(jnp.int32, scores.shape, 1).astype(f32)
    usable = token < counts[: SLOTS * HEADS, :]
    scores = jnp.where(usable, scores, very_low)
    top = jnp.max(scores, axis=1, keepdims=True)
    weights = jnp.where(usable, jnp.exp(scores - top), 0.0)
    total = jnp.sum(weights, axis=1, keepdims=True)
    none = jnp.zeros((8, BLOCK), f32)
    parts = []
    for s in range(0, SLOTS, 2):
        first = jnp.concatenate([weights[s * 8 : s * 8 + 8], none], axis=1)
        second = jnp.concatenate([none, weights[s * 8 + 8 : s * 8 + 16]], axis=1)
        parts.append(
            jnp.dot(
                jnp.concatenate([first, second], axis=0).astype(bf16),
                (values if s < 32 else other_values)[s % 32 : s % 32 + 2].reshape(2 * BLOCK, HD),
                preferred_element_type=f32,
            )
        )
    alive = total > 0.0
    safe = jnp.where(alive, total, 1.0)
    rows[: SLOTS * HEADS, :] = jnp.concatenate(parts, axis=0) / safe
    lse = jnp.where(alive, top + jnp.log(safe), very_low)
    high = lse.astype(bf16).astype(f32)
    mid = (lse - high).astype(bf16).astype(f32)
    low = lse - high - mid
    lane = lax.broadcasted_iota(jnp.int32, (SLOTS * HEADS, HD), 1)
    head = lax.broadcasted_iota(jnp.int32, (SLOTS * HEADS, HD), 0) & 7
    note = jnp.where(
        lane == head,
        high,
        jnp.where(lane == head + 8, mid, jnp.where(lane == head + 16, low, 0.0)),
    )
    note = jnp.sum(note.reshape(SLOTS, HEADS, HD), axis=1)
    side = jnp.concatenate(
        [rows[pl.ds(h, SLOTS, stride=HEADS), :] for h in range(HEADS)] + [note], axis=1
    ).astype(bf16)
    back = jnp.dot(pick[:, :SLOTS], side, preferred_element_type=f32)
    put_items(buf, back)
    out[...] = buf[:ROWS, :].astype(bf16)


def merge_kernel(where_to, items, out, buf):
    buf[:ROWS, :] = items[...].astype(f32)
    by_entry = jnp.dot(where_to[...], get_items(buf).astype(bf16), preferred_element_type=f32)
    blocks = [by_entry[b * REQS : (b + 1) * REQS] for b in range(MAXB)]
    lses = []
    for block in blocks:
        note = block[:, HEADS * HD :]
        lses.append(note[:, :8] + note[:, 8:16] + note[:, 16:24])
    top = jnp.maximum(jnp.maximum(lses[0], lses[1]), jnp.maximum(lses[2], lses[3]))
    scales = [jnp.exp(v - top) for v in lses]
    total = scales[0] + scales[1] + scales[2] + scales[3]
    scales = [v / total for v in scales]
    whole = []
    for h in range(HEADS):
        at = slice(h * HD, (h + 1) * HD)
        whole.append(sum(v[:, h : h + 1] * block[:, at] for v, block in zip(scales, blocks)))
    whole = jnp.concatenate(whole, axis=1)
    out[...] = jnp.concatenate([whole] * 32, axis=0).astype(bf16)


def stage_kernel(*refs):
    n = (len(refs) - 1) // 2
    sources, targets, sems = refs[:n], refs[n : 2 * n], refs[-1]
    copies = []
    for a in range(n):
        step = sources[a].shape[0] // 4
        for k in range(4):
            part = pl.ds(k * step, step)
            copies.append(
                pltpu.make_async_copy(sources[a].at[part], targets[a].at[part], sems.at[a * 4 + k])
            )
    for copy in copies:
        copy.start()
    for copy in copies:
        copy.wait()


def stage(*arrays, name):
    return pl.pallas_call(
        stage_kernel,
        out_shape=tuple(jax.ShapeDtypeStruct(a.shape, a.dtype) for a in arrays),
        in_specs=[HBM] * len(arrays),
        out_specs=(VMEM,) * len(arrays),
        scratch_shapes=[pltpu.SemaphoreType.DMA((4 * len(arrays),))],
        compiler_params=limit,
        cost_estimate=pl.CostEstimate(flops=0, bytes_accessed=1 << 22, transcendentals=0),
        name=name,
    )(*arrays)


def project_kernel(attention, own, other, out):
    me = lax.axis_index("c")
    left = attention[...]
    for c, weight in ((me, own), (1 - me, other)):
        part = jnp.dot(left, weight[...], preferred_element_type=f32)
        part = part.reshape(4, 8, 8, HD)
        part = jnp.concatenate([part[x, z] for z in range(8) for x in range(4)])
        out[pl.ds(pl.multiple_of(c * 256, 256), 256), :] = part.astype(bf16)


def total_kernel(parts, out):
    got = jnp.sum(parts[...].astype(f32).reshape(2, 8, 4, 8, HD), axis=1)
    out[...] = jnp.concatenate([got[c, x] for x in range(4) for c in range(2)]).astype(bf16)


def per_device(queries, pool_keys, pool_values, block_table, ctx_len, out_weight):
    inst = ("z", "x")
    send, where_to = pl.pallas_call(
        route_kernel,
        out_shape=(
            jax.ShapeDtypeStruct((ROWS, HD), bf16),
            jax.ShapeDtypeStruct((REQS * MAXB, HD), bf16),
        ),
        in_specs=[VMEM, VMEM, VMEM],
        out_specs=(VMEM, VMEM),
        scratch_shapes=[pltpu.VMEM((ROWS + 64, HD), f32)],
        compiler_params=pltpu.CompilerParams(vmem_limit_bytes=ROUTE_LIMIT),
        name="route",
    )(block_table.T, ctx_len[None, :], queries)
    send, pool_keys, pool_values, out_weight = lax.optimization_barrier(
        (send, pool_keys, pool_values, out_weight)
    )
    items = lax.all_to_all(
        send.reshape(PEERS, HEADS + 1, PER, HD), inst, split_axis=0, concat_axis=0, tiled=True
    )
    (keys,), values = stage(pool_keys, name="stage_keys"), pool_values
    swap = lambda v: lax.ppermute(v, "c", [(0, 1), (1, 0)])
    other_keys, other_values, other_weight = swap(pool_keys), swap(pool_values), swap(out_weight)
    pick, by_slot = pl.pallas_call(
        unpack_kernel,
        out_shape=(
            jax.ShapeDtypeStruct((PER * PEERS, HD), bf16),
            jax.ShapeDtypeStruct((SLOTS, (HEADS + 1) * HD), f32),
        ),
        in_specs=[VMEM],
        out_specs=(VMEM, VMEM),
        scratch_shapes=[pltpu.VMEM((ROWS + 64, HD), f32)],
        compiler_params=limit,
        cost_estimate=pl.CostEstimate(flops=17179869184, bytes_accessed=67108864, transcendentals=0),
        name="unpack",
    )(items.reshape(ROWS, HD))
    pick, by_slot, other_keys, other_values = lax.optimization_barrier(
        (pick, by_slot, other_keys, other_values)
    )
    back = pl.pallas_call(
        attend_kernel,
        out_shape=jax.ShapeDtypeStruct((ROWS, HD), bf16),
        in_specs=[VMEM] * 6,
        out_specs=VMEM,
        scratch_shapes=[
            pltpu.VMEM((ROWS + 64, HD), f32),
            pltpu.VMEM((SLOTS * HEADS + 16, HD), f32),
            pltpu.VMEM((SLOTS * HEADS + 16, HD), f32),
        ],
        compiler_params=limit,
        name="attend",
    )(pick, by_slot, keys, values, other_keys, other_values)
    partials = lax.all_to_all(
        back.reshape(PEERS, HEADS + 1, PER, HD), inst, split_axis=0, concat_axis=0, tiled=True
    )
    attention = pl.pallas_call(
        merge_kernel,
        out_shape=jax.ShapeDtypeStruct((32 * REQS, HEADS * HD), bf16),
        in_specs=[VMEM, VMEM],
        out_specs=VMEM,
        scratch_shapes=[pltpu.VMEM((ROWS + 64, HD), f32)],
        compiler_params=limit,
        name="merge",
    )(where_to, partials.reshape(ROWS, HD))
    gathered = lax.all_to_all(
        attention.reshape(32, REQS, HEADS * HD), ("x", "z"), split_axis=0, concat_axis=0, tiled=True
    )
    parts = pl.pallas_call(
        project_kernel,
        out_shape=jax.ShapeDtypeStruct((512, HD), bf16),
        in_specs=[VMEM] * 3,
        out_specs=VMEM,
        compiler_params=limit,
        name="project",
    )(gathered.reshape(256, HEADS * HD), out_weight, other_weight)
    swapped = lax.all_to_all(
        parts.reshape(16, 32, HD), ("c", "tp"), split_axis=0, concat_axis=0, tiled=True
    )
    return pl.pallas_call(
        total_kernel,
        out_shape=jax.ShapeDtypeStruct((64, HD), bf16),
        in_specs=[VMEM],
        out_specs=VMEM,
        compiler_params=limit,
        name="total",
    )(swapped.reshape(512, HD))


def solution(mesh):
    split = Mesh(mesh.devices.reshape(8, 4, 2, 8), ("z", "x", "c", "tp"))
    inst = ("z", "x", "c")
    in_specs = (
        P(inst, "tp"),
        P(inst, None, "tp"),
        P(inst, None, "tp"),
        P(inst, None),
        P(inst),
        P("tp", inst),
    )
    return jax.shard_map(
        per_device, mesh=split, in_specs=in_specs, out_specs=P("tp", inst), check_vma=False
    )
```

```python
import jax
import jax.numpy as jnp
from jax import lax
from jax.experimental import pallas as pl
from jax.experimental.pallas import tpu as pltpu
from jax.sharding import Mesh, PartitionSpec as P

HD = 128
BLOCK = 128
MAXB = 4
SLOTS = 64
HEADS = 8
REQS = 8
PEERS = 32
PER = 4
MSG = 9 * PER
ROWS = PEERS * MSG
ROUTE_LIMIT = 60 * 1024 * 1024
very_low = -1e30
f32 = jnp.float32
bf16 = jnp.bfloat16

VMEM = pl.BlockSpec(memory_space=pltpu.VMEM)
HBM = pl.BlockSpec(memory_space=pltpu.HBM)
limit = pltpu.CompilerParams(vmem_limit_bytes=16 * 1024 * 1024)


def put_items(buf, items):
    for i in range(PER):
        for j in range(HEADS + 1):
            buf[pl.ds(PER * j + i, PEERS, stride=MSG), :] = items[
                i * PEERS : (i + 1) * PEERS, j * HD : (j + 1) * HD
            ]


def get_items(buf):
    return jnp.concatenate(
        [
            jnp.concatenate(
                [buf[pl.ds(PER * j + i, PEERS, stride=MSG), :] for j in range(HEADS + 1)], axis=1
            )
            for i in range(PER)
        ],
        axis=0,
    )


def route_kernel(table, ctx, q, out, where_to, buf):
    entries = REQS * MAXB
    row = lax.broadcasted_iota(jnp.int32, (entries, HD), 0)
    lane = lax.broadcasted_iota(jnp.int32, (entries, HD), 1)
    slot = jnp.concatenate(
        [jnp.broadcast_to(table[b : b + 1, :], (REQS, REQS)) for b in range(MAXB)], axis=0
    )
    length = jnp.broadcast_to(ctx[...], (entries, REQS))
    own = lane[:, :REQS] == (row[:, :REQS] & 7)
    slot = jnp.sum(jnp.where(own, slot, 0), axis=1, keepdims=True)
    length = jnp.sum(jnp.where(own, length, 0), axis=1, keepdims=True)
    slot = jnp.broadcast_to(slot, (entries, HD))
    count = jnp.clip(jnp.broadcast_to(length, (entries, HD)) - (row >> 3) * BLOCK, 0, BLOCK)
    inst = slot >> 5
    holder = inst.astype(f32)
    holders = jnp.sum(jnp.where(row == lane, holder, 0.0), axis=0, keepdims=True)
    earlier = jnp.where((holder == holders) & (lane < row), 1.0, 0.0)
    away = (inst & 1) ^ lax.axis_index("c")
    place = (away * 2 * PEERS + ((inst >> 1) & 3) * 8 + (inst >> 3)).astype(f32)
    item = jnp.sum(earlier, axis=1, keepdims=True) * PEERS + place
    pick = jnp.where(lane.astype(f32) == item, 1.0, 0.0).astype(bf16)
    where_to[...] = pick
    note = jnp.where(lane == 0, away * 32 + (slot & 31) + 1, jnp.where(lane == 1, count, 0)).astype(f32)
    side = jnp.concatenate([jnp.concatenate([q[...].astype(f32)] * MAXB, axis=0), note], axis=1)
    items = lax.dot_general(
        pick, side.astype(bf16), (((0,), (0,)), ((), ())), preferred_element_type=f32
    )
    put_items(buf, items)
    out[...] = buf[:ROWS, :].astype(bf16)


def unpack_kernel(items, picks, slots, buf):
    buf[:ROWS, :] = items[...].astype(f32)
    given = get_items(buf)
    queries, notes = given[:, : HEADS * HD], given[:, HEADS * HD :]
    slot_no = lax.broadcasted_iota(jnp.int32, (PER * PEERS, HD), 1).astype(f32) + 1.0
    pick = jnp.where(slot_no == notes[:, :1], 1.0, 0.0).astype(bf16)
    side = jnp.concatenate(
        [queries, jnp.broadcast_to(notes[:, 1:2], (PER * PEERS, HD))], axis=1
    ).astype(bf16)
    by_slot = lax.dot_general(
        pick[:, :SLOTS], side, (((0,), (0,)), ((), ())), preferred_element_type=f32
    )
    picks[...] = pick
    slots[...] = by_slot


def attend_kernel(pick, by_slot, keys, values, other_keys, other_values, out, buf, rows, counts):
    for h in range(HEADS):
        rows[pl.ds(h, SLOTS, stride=HEADS), :] = by_slot[:, h * HD : (h + 1) * HD]
        counts[pl.ds(h, SLOTS, stride=HEADS), :] = by_slot[:, HEADS * HD :]
    parts = []
    for s in range(0, SLOTS, 2):
        pair = lax.dot_general(
            rows[s * 8 : s * 8 + 16, :].astype(bf16),
            (keys if s < 32 else other_keys)[s % 32 : s % 32 + 2].reshape(2 * BLOCK, HD),
            (((1,), (1,)), ((), ())),
            preferred_element_type=f32,
        )
        parts += [pair[:8, :BLOCK], pair[8:, BLOCK:]]
    scores = jnp.concatenate(parts, axis=0) * HD ** (-0.5)
    token = lax.broadcasted_iota(jnp.int32, scores.shape, 1).astype(f32)
    usable = token < counts[: SLOTS * HEADS, :]
    scores = jnp.where(usable, scores, very_low)
    top = jnp.max(scores, axis=1, keepdims=True)
    weights = jnp.where(usable, jnp.exp(scores - top), 0.0)
    total = jnp.sum(weights, axis=1, keepdims=True)
    none = jnp.zeros((8, BLOCK), f32)
    parts = []
    for s in range(0, SLOTS, 2):
        first = jnp.concatenate([weights[s * 8 : s * 8 + 8], none], axis=1)
        second = jnp.concatenate([none, weights[s * 8 + 8 : s * 8 + 16]], axis=1)
        parts.append(
            jnp.dot(
                jnp.concatenate([first, second], axis=0).astype(bf16),
                (values if s < 32 else other_values)[s % 32 : s % 32 + 2].reshape(2 * BLOCK, HD),
                preferred_element_type=f32,
            )
        )
    alive = total > 0.0
    safe = jnp.where(alive, total, 1.0)
    rows[: SLOTS * HEADS, :] = jnp.concatenate(parts, axis=0) / safe
    lse = jnp.where(alive, top + jnp.log(safe), very_low)
    high = lse.astype(bf16).astype(f32)
    mid = (lse - high).astype(bf16).astype(f32)
    low = lse - high - mid
    lane = lax.broadcasted_iota(jnp.int32, (SLOTS * HEADS, HD), 1)
    head = lax.broadcasted_iota(jnp.int32, (SLOTS * HEADS, HD), 0) & 7
    note = jnp.where(
        lane == head,
        high,
        jnp.where(lane == head + 8, mid, jnp.where(lane == head + 16, low, 0.0)),
    )
    note = jnp.sum(note.reshape(SLOTS, HEADS, HD), axis=1)
    side = jnp.concatenate(
        [rows[pl.ds(h, SLOTS, stride=HEADS), :] for h in range(HEADS)] + [note], axis=1
    ).astype(bf16)
    back = jnp.dot(pick[:, :SLOTS], side, preferred_element_type=f32)
    put_items(buf, back)
    out[...] = buf[:ROWS, :].astype(bf16)


def merge_kernel(where_to, items, out, buf):
    buf[:ROWS, :] = items[...].astype(f32)
    by_entry = jnp.dot(where_to[...], get_items(buf).astype(bf16), preferred_element_type=f32)
    blocks = [by_entry[b * REQS : (b + 1) * REQS] for b in range(MAXB)]
    lses = []
    for block in blocks:
        note = block[:, HEADS * HD :]
        lses.append(note[:, :8] + note[:, 8:16] + note[:, 16:24])
    top = jnp.maximum(jnp.maximum(lses[0], lses[1]), jnp.maximum(lses[2], lses[3]))
    scales = [jnp.exp(v - top) for v in lses]
    total = scales[0] + scales[1] + scales[2] + scales[3]
    scales = [v / total for v in scales]
    whole = []
    for h in range(HEADS):
        at = slice(h * HD, (h + 1) * HD)
        whole.append(sum(v[:, h : h + 1] * block[:, at] for v, block in zip(scales, blocks)))
    whole = jnp.concatenate(whole, axis=1)
    out[...] = jnp.concatenate([whole] * 32, axis=0).astype(bf16)


def stage_kernel(*refs):
    n = (len(refs) - 1) // 2
    sources, targets, sems = refs[:n], refs[n : 2 * n], refs[-1]
    copies = []
    for a in range(n):
        step = sources[a].shape[0] // 4
        for k in range(4):
            part = pl.ds(k * step, step)
            copies.append(
                pltpu.make_async_copy(sources[a].at[part], targets[a].at[part], sems.at[a * 4 + k])
            )
    for copy in copies:
        copy.start()
    for copy in copies:
        copy.wait()


def stage(*arrays, name):
    return pl.pallas_call(
        stage_kernel,
        out_shape=tuple(jax.ShapeDtypeStruct(a.shape, a.dtype) for a in arrays),
        in_specs=[HBM] * len(arrays),
        out_specs=(VMEM,) * len(arrays),
        scratch_shapes=[pltpu.SemaphoreType.DMA((4 * len(arrays),))],
        compiler_params=limit,
        cost_estimate=pl.CostEstimate(flops=0, bytes_accessed=1 << 22, transcendentals=0),
        name=name,
    )(*arrays)


def project_kernel(attention, own, other, out):
    me = lax.axis_index("c")
    left = attention[...]
    for c, weight in ((me, own), (1 - me, other)):
        part = jnp.dot(left, weight[...], preferred_element_type=f32)
        part = part.reshape(4, 8, 8, HD)
        part = jnp.concatenate([part[x, z] for z in range(8) for x in range(4)])
        out[pl.ds(pl.multiple_of(c * 256, 256), 256), :] = part.astype(bf16)


def total_kernel(parts, out):
    got = jnp.sum(parts[...].astype(f32).reshape(2, 8, 4, 8, HD), axis=1)
    out[...] = jnp.concatenate([got[c, x] for x in range(4) for c in range(2)]).astype(bf16)


def per_device(queries, pool_keys, pool_values, block_table, ctx_len, out_weight):
    inst = ("x", "z")
    send, where_to = pl.pallas_call(
        route_kernel,
        out_shape=(
            jax.ShapeDtypeStruct((ROWS, HD), bf16),
            jax.ShapeDtypeStruct((REQS * MAXB, HD), bf16),
        ),
        in_specs=[VMEM, VMEM, VMEM],
        out_specs=(VMEM, VMEM),
        scratch_shapes=[pltpu.VMEM((ROWS + 64, HD), f32)],
        compiler_params=pltpu.CompilerParams(vmem_limit_bytes=ROUTE_LIMIT),
        name="route",
    )(block_table.T, ctx_len[None, :], queries)
    send, pool_keys, pool_values, out_weight = lax.optimization_barrier(
        (send, pool_keys, pool_values, out_weight)
    )
    items = lax.all_to_all(
        send.reshape(PEERS, HEADS + 1, PER, HD), inst, split_axis=0, concat_axis=0, tiled=True
    )
    (keys,), values = stage(pool_keys, name="stage_keys"), pool_values
    swap = lambda v: lax.ppermute(v, "c", [(0, 1), (1, 0)])
    other_keys, other_values, other_weight = swap(pool_keys), swap(pool_values), swap(out_weight)
    pick, by_slot = pl.pallas_call(
        unpack_kernel,
        out_shape=(
            jax.ShapeDtypeStruct((PER * PEERS, HD), bf16),
            jax.ShapeDtypeStruct((SLOTS, (HEADS + 1) * HD), f32),
        ),
        in_specs=[VMEM],
        out_specs=(VMEM, VMEM),
        scratch_shapes=[pltpu.VMEM((ROWS + 64, HD), f32)],
        compiler_params=limit,
        cost_estimate=pl.CostEstimate(flops=17179869184, bytes_accessed=67108864, transcendentals=0),
        name="unpack",
    )(items.reshape(ROWS, HD))
    pick, by_slot, other_keys, other_values = lax.optimization_barrier(
        (pick, by_slot, other_keys, other_values)
    )
    back = pl.pallas_call(
        attend_kernel,
        out_shape=jax.ShapeDtypeStruct((ROWS, HD), bf16),
        in_specs=[VMEM] * 6,
        out_specs=VMEM,
        scratch_shapes=[
            pltpu.VMEM((ROWS + 64, HD), f32),
            pltpu.VMEM((SLOTS * HEADS + 16, HD), f32),
            pltpu.VMEM((SLOTS * HEADS + 16, HD), f32),
        ],
        compiler_params=limit,
        name="attend",
    )(pick, by_slot, keys, values, other_keys, other_values)
    partials = lax.all_to_all(
        back.reshape(PEERS, HEADS + 1, PER, HD), inst, split_axis=0, concat_axis=0, tiled=True
    )
    attention = pl.pallas_call(
        merge_kernel,
        out_shape=jax.ShapeDtypeStruct((32 * REQS, HEADS * HD), bf16),
        in_specs=[VMEM, VMEM],
        out_specs=VMEM,
        scratch_shapes=[pltpu.VMEM((ROWS + 64, HD), f32)],
        compiler_params=limit,
        name="merge",
    )(where_to, partials.reshape(ROWS, HD))
    gathered = lax.all_to_all(
        attention.reshape(32, REQS, HEADS * HD), ("x", "z"), split_axis=0, concat_axis=0, tiled=True
    )
    parts = pl.pallas_call(
        project_kernel,
        out_shape=jax.ShapeDtypeStruct((512, HD), bf16),
        in_specs=[VMEM] * 3,
        out_specs=VMEM,
        compiler_params=limit,
        name="project",
    )(gathered.reshape(256, HEADS * HD), out_weight, other_weight)
    swapped = lax.all_to_all(
        parts.reshape(16, 32, HD), ("c", "tp"), split_axis=0, concat_axis=0, tiled=True
    )
    return pl.pallas_call(
        total_kernel,
        out_shape=jax.ShapeDtypeStruct((64, HD), bf16),
        in_specs=[VMEM],
        out_specs=VMEM,
        compiler_params=limit,
        name="total",
    )(swapped.reshape(512, HD))


def solution(mesh):
    split = Mesh(mesh.devices.reshape(8, 4, 2, 8), ("z", "x", "c", "tp"))
    inst = ("z", "x", "c")
    in_specs = (
        P(inst, "tp"),
        P(inst, None, "tp"),
        P(inst, None, "tp"),
        P(inst, None),
        P(inst),
        P("tp", inst),
    )
    return jax.shard_map(
        per_device, mesh=split, in_specs=in_specs, out_specs=P("tp", inst), check_vma=False
    )
```
